256 devices in a mesh: island: 16 (over x_hi, z), fsdp: 16 (over y, x_lo, core).
Axes of the slice: x: 4 (x_hi: 2, x_lo: 2; x = x_hi * 2 + x_lo), y: 4, z: 8, core: 2. Of those that a mesh axis runs over, the one named last changes fastest.
Arguments:
- pseudo_grad: bfloat16 [16, 3840, 5120], P('island', 'fsdp'), may hold values from -6 to 6
- error_buffer: bfloat16 [16, 3840, 5120], P('island', 'fsdp'), may hold values from -4 to 4
- basis_prev: bfloat16 [3840, 128], P('fsdp'), may hold values from -0.09375 to 0.09375
- master_weights: float32 [3840, 5120], P('fsdp', 'island'), may hold values from -1.2 to 1.2
- outer_momentum: float32 [3840, 5120], P('fsdp', 'island'), may hold values from -6 to 6
Outputs:
- error_next: bfloat16 [16, 3840, 5120], P('island', 'fsdp')
- weights_next: bfloat16 [3840, 5120], P('fsdp')
- master_next: float32 [3840, 5120], P('fsdp', 'island')
- momentum_next: float32 [3840, 5120], P('fsdp', 'island')
The draws below stay inside these ranges and needn't reach their ends.
All inputs are finite; a program needn't handle non-finite values.
Results may differ from the reference program's by a relative error of at most 0.009.
Values may be sent and summed in bfloat16 or wider, within the bound.
No kernel may reach another device: no remote copies, remote signals or barrier semaphores. Data moves between devices by JAX's collectives and lax.ppermute only.
A program may use at most 64 MiB of HBM per device.

```python
import jax
import jax.numpy as jnp
from jax import lax

D = 5120
F = 3840
R = 128
ISLANDS = 16
N_ISLAND = 16


def with_spikes(result, stream_key, source, target, parts, factor):
    def block_of(dim):
        return (jnp.arange(result.shape[dim]) // (result.shape[dim] // parts)).reshape((-1,) + (1,) * (result.ndim - 1 - dim))

    one_side = jax.random.permutation(stream_key, parts)[block_of(target)]
    second = (block_of(target) + parts // 2) % parts
    return jnp.where((block_of(source) == one_side) | (block_of(source) == second), factor * result, result)


def steps_of(key, extent, split, least, top_value):
    def one(position, blocks):
        steps = jax.random.uniform(jax.random.fold_in(jax.random.fold_in(key, 6), position), (blocks,), jnp.float32, least / len(split), top_value / len(split))
        return jnp.repeat(jnp.exp(steps), extent[position] // blocks).reshape((-1,) + (1,) * (len(extent) - position - 1))

    level = one(*split[0])
    for cut in split[1:]:
        level = level * one(*cut)
    return level


def normal_values(key, shape, deviation, most, split=(), dtype=jnp.bfloat16):
    values = jax.random.normal(key, shape, jnp.float32) * deviation
    if len(split) > 0:
        values = steps_of(key, shape, split, -0.22, 0.18) * values
    return jnp.clip(values, min=-most, max=most).astype(dtype)


def bell_draw_with(key, shape, deviation, reach, pieces, heavy, kind=jnp.bfloat16):
    values = deviation * jax.random.normal(key, shape, jnp.float32)
    if pieces:
        values = values * steps_of(key, shape, pieces, -0.22, 0.18)
    return jnp.clip(with_spikes(values, jax.random.fold_in(key, 3), *heavy), -reach, reach).astype(kind)


def setup_inputs(seed: int = 0) -> dict:
    streams_of = jax.random.split(jax.random.key(seed), 6)
    pseudo_grad = bell_draw_with(streams_of[0], (ISLANDS, F, D), 1.0, 6.0, ((0, 16), (1, 16)), (1, 2, 16, 2.0))
    error_buffer = normal_values(streams_of[1], (ISLANDS, F, D), 0.5, 4.0, ((0, 16), (1, 16)))
    basis_prev = normal_values(streams_of[2], (F, R), F ** -0.5, 0.09375, ((0, 16),))
    master_weights = normal_values(streams_of[3], (F, D), 0.2, 1.2, ((0, 16), (1, 16)), jnp.float32)
    outer_momentum = normal_values(streams_of[4], (F, D), 1.0, 6.0, ((0, 16), (1, 16)), jnp.float32)
    return {"pseudo_grad": pseudo_grad, "error_buffer": error_buffer, "basis_prev": basis_prev, "master_weights": master_weights, "outer_momentum": outer_momentum}


momentum_coef = 0.9
outer_rate = 0.7

def combine(grad_block, err_block):
    return (grad_block.astype(jnp.float32) + err_block.astype(jnp.float32)).astype(jnp.bfloat16)

def reference(pseudo_grad, error_buffer, basis_prev, master_weights, outer_momentum):

    def add_left(summed, pair):
        merged = combine(pair[0], pair[1])
        return (summed + jnp.dot(merged.T.astype(jnp.float32), basis_prev.astype(jnp.float32), preferred_element_type=jnp.float32), None)
    left_sum = lax.scan(add_left, jnp.zeros((D, R), jnp.float32), (pseudo_grad, error_buffer))[0]
    gram_mat = jnp.dot(left_sum.T.astype(jnp.float32), left_sum.astype(jnp.float32), precision=lax.Precision.HIGHEST, preferred_element_type=jnp.float32)
    factor_low = jnp.linalg.cholesky(gram_mat)
    basis_bf = lax.linalg.triangular_solve(factor_low, left_sum, left_side=False, lower=True, transpose_a=True).astype(jnp.bfloat16)

    def add_right(summed, pair):
        merged = combine(pair[0], pair[1])
        return (summed + jnp.dot(merged.astype(jnp.float32), basis_bf.astype(jnp.float32), preferred_element_type=jnp.float32), None)
    right_sum = lax.scan(add_right, jnp.zeros((F, R), jnp.float32), (pseudo_grad, error_buffer))[0]
    q_avg = (right_sum / N_ISLAND).astype(jnp.bfloat16)
    approx = jnp.dot(q_avg.astype(jnp.float32), basis_bf.T.astype(jnp.float32), preferred_element_type=jnp.float32)

    def new_error(pair):
        merged = combine(pair[0], pair[1])
        return (merged.astype(jnp.float32) - approx).astype(jnp.bfloat16)
    error_next = lax.map(new_error, (pseudo_grad, error_buffer))
    momentum_next = momentum_coef * outer_momentum + approx
    master_next = master_weights - outer_rate * (approx + momentum_coef * momentum_next)
    weights_next = master_next.astype(jnp.bfloat16)
    return (error_next, weights_next, master_next, momentum_next)
```

```python
import jax
import jax.numpy as jnp
from jax import lax
from jax.sharding import Mesh, PartitionSpec as P

momentum_coef = 0.9
outer_rate = 0.7
momentum_part = outer_rate * momentum_coef * momentum_coef
approx_part = outer_rate * (1.0 + momentum_coef)

island = ("xh", "z")
fsdp = ("y", "xl", "core")
plane = ("xh", "y", "xl")


def to_bf(values):
    return values.astype(jnp.bfloat16)


def to_f32(values):
    return values.astype(jnp.float32)


def swap(values, axis, size, bit):
    return lax.ppermute(values, axis, [(place, place ^ bit) for place in range(size)])


def contract_rows(left_mat, right_mat):
    return lax.dot_general(
        left_mat, right_mat, (((0,), (0,)), ((), ())), preferred_element_type=jnp.float32
    )


def contract_columns(left_mat, right_mat, precision=None):
    return lax.dot_general(
        left_mat,
        right_mat,
        (((1,), (1,)), ((), ())),
        precision=precision,
        preferred_element_type=jnp.float32,
    )


def sum_left(partial):
    half = partial.shape[0] // 2
    rank = partial.shape[1]
    core = lax.axis_index("core")
    kept = lax.dynamic_slice_in_dim(partial, core * half, half, 0)
    given = to_bf(lax.dynamic_slice_in_dim(partial, (1 - core) * half, half, 0))
    mine = to_bf(kept + to_f32(swap(given, "core", 2, 1)))
    chunks = lax.all_to_all(mine, plane, 0, 0, tiled=True)
    block = jnp.sum(to_f32(chunks.reshape(16, half // 16, rank)), axis=0)
    for bit in (1, 2, 4):
        block = block + swap(block, "z", 8, bit)
    copies = jnp.broadcast_to(to_bf(block)[None], (16,) + block.shape).reshape(half, rank)
    mine = lax.all_to_all(copies, plane, 0, 0, tiled=True)
    other = swap(mine, "core", 2, 1)
    return jnp.concatenate([jnp.where(core == 0, mine, other), jnp.where(core == 0, other, mine)])


def local(pseudo_grad, error_buffer, basis_prev, master_weights, outer_momentum):
    carried = to_bf(master_weights - momentum_part * outer_momentum)
    carried = lax.all_gather(carried.T, island, axis=0, tiled=True)

    merged = to_bf(to_f32(pseudo_grad[0]) + to_f32(error_buffer[0]))
    left = sum_left(contract_rows(merged, basis_prev))

    product = jnp.dot(merged, left, preferred_element_type=jnp.float32)
    for axis, size, bit in (("xh", 2, 1), ("z", 8, 1), ("z", 8, 2), ("z", 8, 4)):
        product = product + swap(product, axis, size, bit)

    gram_mat = contract_rows(left, left)
    factor_low = jnp.linalg.cholesky(gram_mat)
    inverse_low = lax.linalg.triangular_solve(
        factor_low, jnp.eye(gram_mat.shape[0], dtype=jnp.float32), left_side=True, lower=True
    )
    high = to_bf(inverse_low)
    low = to_bf(inverse_low - to_f32(high))
    basis_bf = to_bf(contract_columns(left, high) + contract_columns(left, low))

    q_avg = to_bf(contract_columns(product, inverse_low, lax.Precision.HIGHEST) / 16)
    approx = contract_columns(q_avg, basis_bf)
    error_next = to_bf(to_f32(merged) - approx)[None]
    weights_next = to_bf(to_f32(carried.T) - approx_part * approx)

    col_count = master_weights.shape[1]
    col_start = lax.axis_index(island) * col_count
    basis_block = lax.dynamic_slice_in_dim(basis_bf, col_start, col_count, 0)
    update = contract_columns(q_avg, basis_block)
    momentum_next = momentum_coef * outer_momentum + update
    master_next = master_weights - outer_rate * (update + momentum_coef * momentum_next)
    return (error_next, weights_next, master_next, momentum_next)


def solution(mesh):
    fine = Mesh(mesh.devices.reshape(2, 8, 4, 2, 2), island + fsdp)
    in_specs = (
        P(island, fsdp, None),
        P(island, fsdp, None),
        P(fsdp, None),
        P(fsdp, island),
        P(fsdp, island),
    )
    out_specs = (
        P(island, fsdp, None),
        P(fsdp, None),
        P(fsdp, island),
        P(fsdp, island),
    )
    return jax.shard_map(local, mesh=fine, in_specs=in_specs, out_specs=out_specs, check_vma=False)
```

```python
import functools

import jax
import jax.numpy as jnp
from jax import lax
from jax.experimental import pallas as pl
from jax.experimental.pallas import tpu as pltpu
from jax.sharding import Mesh, PartitionSpec as P

momentum_coef = 0.9
outer_rate = 0.7
momentum_part = outer_rate * momentum_coef * momentum_coef
approx_part = outer_rate * (1.0 + momentum_coef)

island = ("xh", "z")
fsdp = ("y", "xl", "core")
plane = ("xh", "y", "xl")
panel = 32
whole = pl.BlockSpec(memory_space=pltpu.VMEM)
anywhere = pl.BlockSpec(memory_space=pl.ANY)
scalars = pl.BlockSpec(memory_space=pltpu.SMEM)


def to_bf(values):
    return values.astype(jnp.bfloat16)


def to_f32(values):
    return values.astype(jnp.float32)


def times(left_mat, right_mat, left_dim=1, right_dim=0, precision=None):
    return lax.dot_general(
        left_mat,
        right_mat,
        (((left_dim,), (right_dim,)), ((), ())),
        precision=precision,
        preferred_element_type=jnp.float32,
    )


def shaped(shape, dtype):
    return jax.ShapeDtypeStruct(shape, dtype)


def near(shape, dtype):
    return pltpu.VMEM(shape, dtype)


def to_near(values):
    return pltpu.with_memory_space_constraint(values, pltpu.VMEM)


def to_far(values):
    return pltpu.with_memory_space_constraint(values, pltpu.HBM)


def params(size=16):
    return pltpu.CompilerParams(vmem_limit_bytes=size * 2**20)


def cost(flops, size):
    return pl.CostEstimate(flops=flops, bytes_accessed=size, transcendentals=0)


def fetch(source, target, sem):
    copy = pltpu.make_async_copy(source, target, sem)
    copy.start()
    return copy


def project_kernel(pieces, which, grad, error, basis, *rest):
    first = len(rest) > 6
    if first:
        master, momentum, left_out, merged_out, own_out, grads, errors, bases, sems, masters, momenta = rest
    else:
        left_out, merged_out, grads, errors, bases, sems = rest
    half = left_out.shape[1]
    width = half // pieces
    start = which[0] * half
    waits = [fetch(basis, bases, sems.at[0])]
    for piece in range(pieces):
        there = pl.ds(pl.multiple_of(start + piece * width, width), width)
        here = pl.ds(piece * width, width)
        waits.append(fetch(grad.at[:, there], grads.at[:, here], sems.at[1 + 2 * piece]))
        waits.append(fetch(error.at[:, there], errors.at[:, here], sems.at[2 + 2 * piece]))
    if first:
        waits.append(fetch(master, masters, sems.at[1 + 2 * pieces]))
        waits.append(fetch(momentum, momenta, sems.at[2 + 2 * pieces]))
    waits[0].wait()
    turned = to_bf(to_f32(bases[...]).T)
    for piece in range(pieces):
        here = slice(piece * width, (piece + 1) * width)
        waits[1 + 2 * piece].wait()
        waits[2 + 2 * piece].wait()
        merged = to_bf(to_f32(grads[:, here]) + to_f32(errors[:, here]))
        merged_out[:, here] = merged
        left_out[:, here] = times(turned, merged).astype(left_out.dtype)
    if first:
        waits[-2].wait()
        waits[-1].wait()
        own_out[...] = to_bf(masters[...] - momentum_part * momenta[...])


def project(which, grad, error, basis, dtype, master=None, momentum=None):
    rows, cols = grad.shape
    rank = basis.shape[1]
    half = cols // 2
    pieces = 5
    out_shape = [near((rank, half), dtype), near((rows, half), jnp.bfloat16)]
    operands = [which, to_far(grad), to_far(error), to_far(basis)]
    scratch = [
        pltpu.VMEM((rows, half), jnp.bfloat16),
        pltpu.VMEM((rows, half), jnp.bfloat16),
        pltpu.VMEM((rows, rank), jnp.bfloat16),
        pltpu.SemaphoreType.DMA((3 + 2 * pieces,)),
    ]
    if master is not None:
        operands += [to_far(master), to_far(momentum)]
        out_shape.append(near(master.shape, jnp.bfloat16))
        scratch += [pltpu.VMEM(master.shape, jnp.float32)] * 2
    return pl.pallas_call(
        functools.partial(project_kernel, pieces),
        in_specs=[scalars] + [anywhere] * (len(operands) - 1),
        out_specs=[whole] * len(out_shape),
        out_shape=out_shape,
        scratch_shapes=scratch,
        compiler_params=params(24),
        cost_estimate=cost(rows * cols * rank, 2 * rows * cols),
    )(*operands)


def combine_kernel(kept, received, own, across, mine_out, bundle_out):
    mine_out[...] = to_bf(kept[...] + to_f32(received[...]))
    bundle_out[0] = own[...]
    bundle_out[1] = across[...]


def combine(kept, received, own, across):
    return pl.pallas_call(
        combine_kernel,
        in_specs=[whole] * 4,
        out_specs=[whole] * 2,
        out_shape=[near(kept.shape, jnp.bfloat16), near((2,) + own.shape, own.dtype)],
        compiler_params=params(),
        cost_estimate=cost(kept.size, 8 * kept.size),
    )(to_near(kept), received, to_near(own), across)


def sum_kernel(chunks, *rest):
    out = rest[-1]
    total = to_f32(chunks[0])
    for place in range(1, chunks.shape[0]):
        total = total + to_f32(chunks[place])
    out[...] = total


def sum_chunks(chunks, after):
    return pl.pallas_call(
        sum_kernel,
        in_specs=[whole] + [anywhere] * len(after),
        out_specs=whole,
        out_shape=near(chunks.shape[1:], jnp.float32),
        compiler_params=params(),
        cost_estimate=cost(chunks.size, 2 * chunks.size),
    )(chunks, *[to_far(array) for array in after])


def spread_kernel(count, block, arrived, *rest):
    out = rest[-1]
    total = to_bf(block[...] + arrived[...])
    for place in range(count):
        out[place] = total


def spread(block, arrived, count, held):
    outs = pl.pallas_call(
        functools.partial(spread_kernel, count),
        in_specs=[whole, whole] + [anywhere] * len(held),
        out_specs=[anywhere] * len(held) + [whole],
        out_shape=[shaped(array.shape, array.dtype) for array in held]
        + [near((count,) + block.shape, jnp.bfloat16)],
        input_output_aliases={2 + place: place for place in range(len(held))},
        compiler_params=params(),
        cost_estimate=cost(block.size, 2 * count * block.size),
    )(to_near(block), arrived, *[to_far(array) for array in held])
    return outs[-1], outs[:-1]


def product_kernel(first, merged, left, *rest):
    values = left[...]
    product = times(merged[...], values, 1, 1)
    gram_mat = times(values, values, 1, 1)
    if first:
        product_out, gram_out = rest
    else:
        product_out, gram_out = rest[-2:]
        product = rest[0][...] + product
        gram_mat = rest[1][...] + gram_mat
    product_out[...] = product
    gram_out[...] = gram_mat


def product_of(merged, left, before=(), held=()):
    rows = merged.shape[0]
    rank = left.shape[0]
    outs = pl.pallas_call(
        functools.partial(product_kernel, not before),
        in_specs=[whole] * (2 + len(before)) + [anywhere] * len(held),
        out_specs=[anywhere] * len(held) + [whole] * 2,
        out_shape=[shaped(array.shape, array.dtype) for array in held]
        + [near((rows, rank), jnp.float32), near((rank, rank), jnp.float32)],
        input_output_aliases={2 + len(before) + place: place for place in range(len(held))},
        compiler_params=params(),
        cost_estimate=cost(2 * rows * left.size, 4 * left.size),
    )(to_near(merged), left, *[to_near(array) for array in before], *[to_far(array) for array in held])
    return outs[-2:], outs[:-2]


def factor_kernel(start, state, *refs):
    rank = state.shape[0]
    stop = start + panel
    exact = lax.Precision.HIGHEST
    state_out, inverse_out = refs[-2:]
    if start == 0:
        full_row = lax.broadcasted_iota(jnp.int32, (rank, rank), 0)
        full_col = lax.broadcasted_iota(jnp.int32, (rank, rank), 1)
        inverse = jnp.where(full_row == full_col, 1.0, 0.0)
    else:
        inverse = refs[0]
    rows = state[start:stop, :]
    below = inverse[start:stop, :]
    small = rows[:, start:stop]
    row_of = lax.broadcasted_iota(jnp.int32, (panel, panel), 0)
    col_of = lax.broadcasted_iota(jnp.int32, (panel, panel), 1)
    turned = jnp.where(row_of == col_of, 1.0, 0.0)
    for k in range(panel):
        column = small[:, k : k + 1]
        pivot = small[k : k + 1, k : k + 1]
        factor = jnp.where(row_of[:, :1] > k, column / pivot, 0.0)
        small = small - factor * small[k : k + 1, :]
        turned = turned - factor * turned[k : k + 1, :]
    diagonal = jnp.sum(jnp.where(row_of == col_of, small, 0.0), axis=1, keepdims=True)
    turned = turned * lax.rsqrt(diagonal)
    rows = times(turned, rows, precision=exact)
    below = times(turned, below, precision=exact)
    if start > 0:
        inverse_out[0:start, :] = inverse[0:start, :]
    inverse_out[start:stop, :] = below
    if stop < rank:
        later = rows.T[stop:, :]
        state_out[0:stop, :] = state[0:stop, :]
        state_out[stop:, :] = state[stop:, :] - times(later, rows, precision=exact)
        inverse_out[stop:, :] = inverse[stop:, :] - times(later, below, precision=exact)
    else:
        state_out[...] = state[...]


def factor_step(start, state, *inverse):
    rank = state.shape[0]
    return pl.pallas_call(
        functools.partial(factor_kernel, start),
        in_specs=[whole] * (1 + len(inverse)),
        out_specs=[whole, whole],
        out_shape=[near((rank, rank), jnp.float32)] * 2,
        compiler_params=params(),
        cost_estimate=cost(10**9, 4 * rank * rank * 4),
    )(*[to_near(array) for array in (state, *inverse)])


def basis_kernel(which, inverse, mine, other, out):
    half = mine.shape[1]
    value = inverse[...]
    high = to_bf(value)
    low = to_bf(value - to_f32(high))

    def put(left, start):
        left = left[...]
        basis = times(high, left) + times(low, left)
        out[:, pl.ds(pl.multiple_of(start, half), half)] = to_bf(basis)

    put(mine, which[0] * half)
    put(other, (1 - which[0]) * half)


def basis_of(which, inverse, mine, other):
    rank, half = mine.shape
    return pl.pallas_call(
        basis_kernel,
        in_specs=[pl.BlockSpec(memory_space=pltpu.SMEM), whole, whole, whole],
        out_specs=whole,
        out_shape=near((rank, 2 * half), jnp.bfloat16),
        compiler_params=params(),
        cost_estimate=cost(8 * rank * rank * half, 8 * rank * half),
    )(which, to_near(inverse), mine, other)


def final_kernel(
    islands, pieces, which, inverse, product, arrived, basis, merged_mine, merged_other, carried, block, master,
    momentum, error_out, weights_out, master_out, momentum_out, errors, weights, masters, momenta, sems,
):
    total = product[...] + arrived[...]
    q_avg = to_bf(times(total, inverse[...], 1, 1, lax.Precision.HIGHEST) / islands)
    half = merged_mine.shape[1]
    width = half // pieces
    waits = []
    for number, merged in enumerate((merged_mine, merged_other)):
        start = lax.rem(which[0] + number, 2) * half
        for piece in range(pieces):
            lanes = pl.ds(pl.multiple_of(start + piece * width, width), width)
            approx = times(q_avg, basis[:, lanes])
            errors[:, lanes] = to_bf(to_f32(merged[:, piece * width : (piece + 1) * width]) - approx)
            waits.append(fetch(errors.at[:, lanes], error_out.at[:, lanes], sems.at[len(waits)]))
            weights[:, lanes] = to_bf(to_f32(carried[:, lanes]) - approx_part * approx)
            waits.append(fetch(weights.at[:, lanes], weights_out.at[:, lanes], sems.at[len(waits)]))
    update = times(block[...], q_avg, 1, 1)
    momentum_next = momentum_coef * momentum[...] + update
    momenta[...] = momentum_next
    waits.append(fetch(momenta, momentum_out, sems.at[len(waits)]))
    masters[...] = master[...] - outer_rate * (update + momentum_coef * momentum_next)
    waits.append(fetch(masters, master_out, sems.at[len(waits)]))
    for copy in waits:
        copy.wait()


def final(islands, which, inverse, product, arrived, basis, mine, other, carried, block, master, momentum):
    rows, half = mine.shape
    rank = basis.shape[0]
    cols = 2 * half
    own = master.shape
    pieces = 5
    return pl.pallas_call(
        functools.partial(final_kernel, islands, pieces),
        in_specs=[scalars] + [whole] * 10,
        out_specs=[anywhere] * 4,
        out_shape=[
            shaped((rows, cols), jnp.bfloat16),
            shaped((rows, cols), jnp.bfloat16),
            shaped(own, jnp.float32),
            shaped(own, jnp.float32),
        ],
        scratch_shapes=[pltpu.VMEM((rows, cols), jnp.bfloat16)] * 2
        + [pltpu.VMEM(own, jnp.float32)] * 2
        + [pltpu.SemaphoreType.DMA((4 * pieces + 2,))],
        compiler_params=params(24),
        cost_estimate=cost(2 * rows * cols * rank, 8 * rows * cols),
    )(
        which, to_near(inverse), to_near(product), arrived, to_near(basis), to_near(mine), to_near(other),
        to_near(carried), block, master, momentum,
    )


def gather_kernel(shifts, place, _, *refs):
    pieces, out, held, sems = refs[:-3], refs[-3], refs[-2], refs[-1]
    size = pieces[0].shape[1]
    count = len(shifts)
    waits = []
    for number in range(count):
        z_of = lax.rem(place[1] + (shifts[number] + count), count)
        rows = pl.ds(pl.multiple_of(z_of * size, size), size)
        for side in range(2):
            waits.append(fetch(pieces[number].at[side], held.at[side, rows], sems.at[len(waits)]))
    for copy in waits:
        copy.wait()
    span = count * size
    for side in range(2):
        start = lax.rem(place[0] + side, 2) * span
        for first in range(0, span, 2 * size):
            lanes = pl.ds(pl.multiple_of(start + first, 128), 2 * size)
            out[:, lanes] = to_bf(to_f32(held[side, first : first + 2 * size, :]).T)


def gather_pieces(place, pieces, shifts, after):
    rows, cols = pieces[0].shape[1:]
    count = 2 * len(pieces)
    return pl.pallas_call(
        functools.partial(gather_kernel, shifts),
        in_specs=[scalars] + [anywhere] * (1 + len(pieces)),
        out_specs=whole,
        out_shape=near((cols, count * rows), jnp.bfloat16),
        scratch_shapes=[
            pltpu.VMEM((2, len(pieces) * rows, cols), jnp.bfloat16),
            pltpu.SemaphoreType.DMA((count,)),
        ],
        compiler_params=params(),
        cost_estimate=cost(10**9, 4 * count * rows * cols),
    )(place, after, *pieces)


def add_kernel(first, second, *rest):
    rest[-1][...] = first[...] + second[...]


def add_after(first, second, after, held=()):
    outs = pl.pallas_call(
        add_kernel,
        in_specs=[whole, whole, anywhere] + [anywhere] * len(held),
        out_specs=[anywhere] * len(held) + [whole],
        out_shape=[shaped(array.shape, array.dtype) for array in held] + [near(first.shape, first.dtype)],
        input_output_aliases={3 + place: place for place in range(len(held))},
        compiler_params=params(),
        cost_estimate=cost(first.size, 12 * first.size),
    )(to_near(first), second, after, *[to_far(array) for array in held])
    return outs[-1], outs[:-1]


def shift(values, by):
    return lax.ppermute(values, "z", [(place, (place + by) % 8) for place in range(8)])


def swap(values, axis, size, bit):
    return lax.ppermute(values, axis, [(place, place ^ bit) for place in range(size)])


def shift(values, by):
    return lax.ppermute(values, "z", [(place, (place + by) % 8) for place in range(8)])


def local(pseudo_grad, error_buffer, basis_prev, master_weights, outer_momentum):
    core = lax.axis_index("core").astype(jnp.int32)
    rank = basis_prev.shape[1]
    grad, error = pseudo_grad[0], error_buffer[0]
    half = grad.shape[1] // 2
    which_mine, which_other = core.reshape(1), (1 - core).reshape(1)
    place = jnp.stack([lax.axis_index("xh"), lax.axis_index("z")]).astype(jnp.int32)
    master, momentum = master_weights.T, outer_momentum.T

    given, merged_other, own = project(which_other, grad, error, basis_prev, jnp.bfloat16, master, momentum)
    received = swap(given, "core", 2, 1)
    across = swap(own, "xh", 2, 1)
    kept, merged_mine = project(which_mine, grad, error, basis_prev, jnp.float32)
    mine, bundle = combine(kept, received, own, across)
    up, down = shift(bundle, 1), shift(bundle, -1)
    chunks = lax.all_to_all(mine.reshape(16, rank // 16, half), plane, 0, 0, tiled=True)
    block = sum_chunks(chunks, (up, down))
    for bit in (1, 2):
        block = block + swap(block, "z", 8, bit)
    copies, (up, down) = spread(block, swap(block, "z", 8, 4), 16, (up, down))
    pieces = [bundle, up, down]
    up, down = shift(up, 1), shift(down, -1)
    mine = lax.all_to_all(copies, plane, 0, 0, tiled=True).reshape(rank, half)
    other = swap(mine, "core", 2, 1)

    before, _ = product_of(merged_mine, mine)
    (product, gram_mat), (up, down) = product_of(merged_other, other, before, (up, down))
    pieces += [up, down]
    up, down = shift(up, 1), shift(down, -1)

    state, inverse = factor_step(0, gram_mat)
    state, inverse = factor_step(panel, state, inverse)
    product, _ = add_after(product, swap(product, "xh", 2, 1), state)
    state, inverse = factor_step(2 * panel, state, inverse)
    product, (up,) = add_after(product, swap(product, "z", 8, 1), state, (up,))
    pieces += [up, down]
    up = shift(up, 1)
    _, inverse = factor_step(3 * panel, state, inverse)
    basis_bf = basis_of(which_mine, inverse, mine, other)
    product, _ = add_after(product, swap(product, "z", 8, 2), basis_bf)
    pieces.append(up)
    arrived = swap(product, "z", 8, 4)
    carried = gather_pieces(place, pieces, (0, -1, 1, -2, 2, -3, 3, -4), product)

    col_count = master.shape[0]
    col_start = lax.axis_index(island) * col_count
    basis_block = lax.dynamic_slice_in_dim(basis_bf, col_start, col_count, 1).T
    error_next, weights_next, master_next, momentum_next = final(
        16, which_mine, inverse, product, arrived, basis_bf, merged_mine, merged_other, carried, basis_block,
        master, momentum,
    )
    return (error_next[None], weights_next, master_next.T, momentum_next.T)


def solution(mesh):
    fine = Mesh(mesh.devices.reshape(2, 8, 4, 2, 2), island + fsdp)
    in_specs = (
        P(island, fsdp, None),
        P(island, fsdp, None),
        P(fsdp, None),
        P(fsdp, island),
        P(fsdp, island),
    )
    out_specs = (
        P(island, fsdp, None),
        P(fsdp, None),
        P(fsdp, island),
        P(fsdp, island),
    )
    return jax.shard_map(local, mesh=fine, in_specs=in_specs, out_specs=out_specs, check_vma=False)
```

```python
import functools

import jax
import jax.numpy as jnp
from jax import lax
from jax.experimental import pallas as pl
from jax.experimental.pallas import tpu as pltpu
from jax.sharding import Mesh, PartitionSpec as P

momentum_coef = 0.9
outer_rate = 0.7
momentum_part = outer_rate * momentum_coef * momentum_coef
approx_part = outer_rate * (1.0 + momentum_coef)

island = ("xh", "z")
fsdp = ("y", "xl", "core")
plane = ("xh", "y", "xl")
panel = 32
group = 8
whole = pl.BlockSpec(memory_space=pltpu.VMEM)
anywhere = pl.BlockSpec(memory_space=pl.ANY)
scalars = pl.BlockSpec(memory_space=pltpu.SMEM)


def to_bf(values):
    return values.astype(jnp.bfloat16)


def to_f32(values):
    return values.astype(jnp.float32)


def times(left_mat, right_mat, left_dim=1, right_dim=0, precision=None):
    return lax.dot_general(
        left_mat,
        right_mat,
        (((left_dim,), (right_dim,)), ((), ())),
        precision=precision,
        preferred_element_type=jnp.float32,
    )


def shaped(shape, dtype):
    return jax.ShapeDtypeStruct(shape, dtype)


def far(shape, dtype):
    return pltpu.HBM(shape, dtype)


def near(shape, dtype):
    return pltpu.VMEM(shape, dtype)


def to_near(values):
    return pltpu.with_memory_space_constraint(values, pltpu.VMEM)


def to_far(values):
    return pltpu.with_memory_space_constraint(values, pltpu.HBM)


def params(size=16):
    return pltpu.CompilerParams(vmem_limit_bytes=size * 2**20)


def cost(flops, size):
    return pl.CostEstimate(flops=flops, bytes_accessed=size, transcendentals=0)


def fetch(source, target, sem):
    copy = pltpu.make_async_copy(source, target, sem)
    copy.start()
    return copy


def project_kernel(pieces, which, grad, error, basis, *rest):
    first = len(rest) > 6
    if first:
        master, momentum, left_out, merged_out, own_out, grads, errors, bases, sems, masters, momenta = rest
    else:
        left_out, merged_out, grads, errors, bases, sems = rest
    half = left_out.shape[1]
    width = half // pieces
    start = which[0] * half
    waits = [fetch(basis, bases, sems.at[0])]
    for piece in range(pieces):
        there = pl.ds(pl.multiple_of(start + piece * width, width), width)
        here = pl.ds(piece * width, width)
        waits.append(fetch(grad.at[:, there], grads.at[:, here], sems.at[1 + 2 * piece]))
        waits.append(fetch(error.at[:, there], errors.at[:, here], sems.at[2 + 2 * piece]))
    if first:
        waits.append(fetch(master, masters, sems.at[1 + 2 * pieces]))
        waits.append(fetch(momentum, momenta, sems.at[2 + 2 * pieces]))
    waits[0].wait()
    turned = to_bf(to_f32(bases[...]).T)
    for piece in range(pieces):
        here = slice(piece * width, (piece + 1) * width)
        waits[1 + 2 * piece].wait()
        waits[2 + 2 * piece].wait()
        merged = to_bf(to_f32(grads[:, here]) + to_f32(errors[:, here]))
        merged_out[:, here] = merged
        left_out[:, here] = times(turned, merged).astype(left_out.dtype)
    if first:
        waits[-2].wait()
        waits[-1].wait()
        own_out[...] = to_bf(masters[...] - momentum_part * momenta[...])


def project(which, grad, error, basis, dtype, master=None, momentum=None):
    rows, cols = grad.shape
    rank = basis.shape[1]
    half = cols // 2
    pieces = 5
    out_shape = [near((rank, half), dtype), near((rows, half), jnp.bfloat16)]
    operands = [which, to_far(grad), to_far(error), to_far(basis)]
    scratch = [
        pltpu.VMEM((rows, half), jnp.bfloat16),
        pltpu.VMEM((rows, half), jnp.bfloat16),
        pltpu.VMEM((rows, rank), jnp.bfloat16),
        pltpu.SemaphoreType.DMA((3 + 2 * pieces,)),
    ]
    if master is not None:
        operands += [to_far(master), to_far(momentum)]
        out_shape.append(near(master.shape, jnp.bfloat16))
        scratch += [pltpu.VMEM(master.shape, jnp.float32)] * 2
    return pl.pallas_call(
        functools.partial(project_kernel, pieces),
        in_specs=[scalars] + [anywhere] * (len(operands) - 1),
        out_specs=[whole] * len(out_shape),
        out_shape=out_shape,
        scratch_shapes=scratch,
        compiler_params=params(24),
        cost_estimate=cost(rows * cols * rank, 2 * rows * cols),
    )(*operands)


def combine_kernel(kept, received, own, across, mine_out, bundle_out):
    mine_out[...] = to_bf(kept[...] + to_f32(received[...]))
    bundle_out[0] = own[...]
    bundle_out[1] = across[...]


def combine(kept, received, own, across):
    return pl.pallas_call(
        combine_kernel,
        in_specs=[whole] * 4,
        out_specs=[whole] * 2,
        out_shape=[near(kept.shape, jnp.bfloat16), near((2,) + own.shape, own.dtype)],
        compiler_params=params(),
        cost_estimate=cost(kept.size, 8 * kept.size),
    )(to_near(kept), received, to_near(own), across)


def sum_kernel(chunks, *rest):
    out = rest[-1]
    total = to_f32(chunks[0])
    for place in range(1, chunks.shape[0]):
        total = total + to_f32(chunks[place])
    out[...] = to_bf(total)


def sum_chunks(chunks, after):
    return pl.pallas_call(
        sum_kernel,
        in_specs=[whole] + [anywhere] * len(after),
        out_specs=whole,
        out_shape=near(chunks.shape[1:], jnp.bfloat16),
        compiler_params=params(),
        cost_estimate=cost(chunks.size, 2 * chunks.size),
    )(chunks, *[to_far(array) for array in after])


def spread_kernel(count, block, arrived, *rest):
    out = rest[-1]
    total = to_bf(to_f32(block[...]) + to_f32(arrived[...]))
    for place in range(count):
        out[place] = total


def spread(block, arrived, count, held):
    outs = pl.pallas_call(
        functools.partial(spread_kernel, count),
        in_specs=[whole, whole] + [anywhere] * len(held),
        out_specs=[anywhere] * len(held) + [whole],
        out_shape=[far(array.shape, array.dtype) for array in held]
        + [far((count,) + block.shape, jnp.bfloat16)],
        input_output_aliases={2 + place: place for place in range(len(held))},
        compiler_params=params(),
        cost_estimate=cost(block.size, 2 * count * block.size),
    )(to_near(block), arrived, *[to_far(array) for array in held])
    return outs[-1], outs[:-1]


def product_kernel(first, merged, left, *rest):
    values = left[...]
    product = times(merged[...], values, 1, 1)
    gram_mat = times(values, values, 1, 1)
    product_out, gram_out = rest[-2:]
    if not first:
        product = rest[0][...] + product
        gram_mat = rest[1][...] + gram_mat
    product_out[...] = product.astype(product_out.dtype)
    gram_out[...] = gram_mat


def product_of(merged, left, before=(), held=()):
    rows = merged.shape[0]
    rank = left.shape[0]
    outs = pl.pallas_call(
        functools.partial(product_kernel, not before),
        in_specs=[whole] * (2 + len(before)) + [anywhere] * len(held),
        out_specs=[anywhere] * len(held) + [whole] * 2,
        out_shape=[far(array.shape, array.dtype) for array in held]
        + [near((rows, rank), jnp.bfloat16 if before else jnp.float32), near((rank, rank), jnp.float32)],
        input_output_aliases={2 + len(before) + place: place for place in range(len(held))},
        compiler_params=params(),
        cost_estimate=cost(2 * rows * left.size, 4 * left.size),
    )(to_near(merged), to_near(left), *[to_near(array) for array in before], *[to_far(array) for array in held])
    return outs[-2:], outs[:-2]


def factor_kernel(gram_mat, inverse_out, state, below_all):
    rank = gram_mat.shape[0]
    exact = lax.Precision.HIGHEST
    row_of = lax.broadcasted_iota(jnp.int32, (rank, rank), 0)
    col_of = lax.broadcasted_iota(jnp.int32, (rank, rank), 1)
    state[...] = gram_mat[...]
    below_all[...] = jnp.where(row_of == col_of, 1.0, 0.0)
    row_of, col_of = row_of[:panel], col_of[:panel]
    for start in range(0, rank, panel):
        stop = start + panel
        rows, below = state[start:stop, :], below_all[start:stop, :]
        for first in range(0, panel, group):
            columns = [
                jnp.broadcast_to(rows[:, start + k : start + k + 1], (panel, rank))
                for k in range(first, first + group)
            ]
            for place in range(group):
                k = first + place
                factor = jnp.where(row_of > k, columns[place], 0.0) * (1.0 / columns[place][k : k + 1, :])
                for later in range(place + 1, group):
                    columns[later] = columns[later] - factor * columns[later][k : k + 1, :]
                rows = rows - factor * rows[k : k + 1, :]
                below = below - factor * below[k : k + 1, :]
        diagonal = jnp.sum(jnp.where(col_of == row_of + start, rows, 0.0), axis=1, keepdims=True)
        scale = lax.rsqrt(diagonal)
        rows, below = rows * scale, below * scale
        inverse_out[start:stop, :] = below
        if stop < rank:
            later = rows.T[stop:, :]
            state[stop:, :] -= times(later, rows, precision=exact)
            below_all[stop:, :] -= times(later, below, precision=exact)


def inverse_factor(gram_mat):
    rank = gram_mat.shape[0]
    return pl.pallas_call(
        factor_kernel,
        in_specs=[whole],
        out_specs=whole,
        out_shape=near((rank, rank), jnp.float32),
        scratch_shapes=[pltpu.VMEM((rank, rank), jnp.float32)] * 2,
        compiler_params=params(),
        cost_estimate=cost(10**9, 4 * rank * rank * 4),
    )(to_near(gram_mat))


def basis_kernel(which, side, depth, inverse, mine, other, _, out, block_out, held):
    half = mine.shape[1]
    value = inverse[...]
    high = to_bf(value)
    low = to_bf(value - to_f32(high))

    def put(left, start):
        left = left[...]
        basis = times(high, left) + times(low, left)
        out[:, pl.ds(pl.multiple_of(start, half), half)] = to_bf(basis)

    put(mine, which[0] * half)
    put(other, (1 - which[0]) * half)
    size = block_out.shape[0]
    pair = side[0] * half + (depth[0] // 2) * (2 * size)
    held[...] = to_f32(out[:, pl.ds(pl.multiple_of(pair, 2 * size), 2 * size)]).T
    block_out[...] = to_bf(held[pl.ds(pl.multiple_of(lax.rem(depth[0], 2) * size, size), size), :])


def basis_of(which, side, depth, inverse, mine, other, size, after):
    rank, half = mine.shape
    return pl.pallas_call(
        basis_kernel,
        in_specs=[scalars] * 3 + [whole] * 3 + [anywhere],
        out_specs=[whole] * 2,
        out_shape=[near((rank, 2 * half), jnp.bfloat16), near((size, rank), jnp.bfloat16)],
        scratch_shapes=[pltpu.VMEM((2 * size, rank), jnp.float32)],
        compiler_params=params(),
        cost_estimate=cost(8 * rank * rank * half, 8 * rank * half),
    )(which, side, depth, to_near(inverse), to_near(mine), to_near(other), after)


def final_kernel(
    islands, pieces, which, inverse, product, arrived, basis, merged_mine, merged_other, carried, block, master,
    momentum, error_out, weights_out, master_out, momentum_out, errors, weights, masters, momenta, sems,
):
    total = to_f32(product[...]) + to_f32(arrived[...])
    q_avg = to_bf(times(total, inverse[...], 1, 1, lax.Precision.HIGHEST) / islands)
    half = merged_mine.shape[1]
    width = half // pieces
    waits = []
    for number, merged in enumerate((merged_mine, merged_other)):
        start = lax.rem(which[0] + number, 2) * half
        for piece in range(pieces):
            lanes = pl.ds(pl.multiple_of(start + piece * width, width), width)
            approx = times(q_avg, basis[:, lanes])
            errors[:, lanes] = to_bf(to_f32(merged[:, piece * width : (piece + 1) * width]) - approx)
            waits.append(fetch(errors.at[:, lanes], error_out.at[:, lanes], sems.at[len(waits)]))
            weights[:, lanes] = to_bf(to_f32(carried[:, lanes]) - approx_part * approx)
            waits.append(fetch(weights.at[:, lanes], weights_out.at[:, lanes], sems.at[len(waits)]))
    update = times(block[...], q_avg, 1, 1)
    momentum_next = momentum_coef * momentum[...] + update
    momenta[...] = momentum_next
    waits.append(fetch(momenta, momentum_out, sems.at[len(waits)]))
    masters[...] = master[...] - outer_rate * (update + momentum_coef * momentum_next)
    waits.append(fetch(masters, master_out, sems.at[len(waits)]))
    for copy in waits:
        copy.wait()


def final(islands, which, inverse, product, arrived, basis, mine, other, carried, block, master, momentum):
    rows, half = mine.shape
    rank = basis.shape[0]
    cols = 2 * half
    own = master.shape
    pieces = 5
    return pl.pallas_call(
        functools.partial(final_kernel, islands, pieces),
        in_specs=[scalars] + [whole] * 10,
        out_specs=[anywhere] * 4,
        out_shape=[
            shaped((rows, cols), jnp.bfloat16),
            shaped((rows, cols), jnp.bfloat16),
            shaped(own, jnp.float32),
            shaped(own, jnp.float32),
        ],
        scratch_shapes=[pltpu.VMEM((rows, cols), jnp.bfloat16)] * 2
        + [pltpu.VMEM(own, jnp.float32)] * 2
        + [pltpu.SemaphoreType.DMA((4 * pieces + 2,))],
        compiler_params=params(24),
        cost_estimate=cost(2 * rows * cols * rank, 8 * rows * cols),
    )(
        which, to_near(inverse), to_near(product), to_near(arrived), to_near(basis), to_near(mine), to_near(other),
        to_near(carried), to_near(block), master, momentum,
    )


def gather_kernel(shifts, side_of, depth, _, *refs):
    pieces, out, held, sems = refs[:-3], refs[-3], refs[-2], refs[-1]
    size = pieces[0].shape[1]
    count = len(shifts)
    waits = []
    for number in range(count):
        z_of = lax.rem(depth[0] + (shifts[number] + count), count)
        rows = pl.ds(pl.multiple_of(z_of * size, size), size)
        for side in range(2):
            waits.append(fetch(pieces[number].at[side], held.at[side, rows], sems.at[len(waits)]))
    for copy in waits:
        copy.wait()
    span = count * size
    for side in range(2):
        start = lax.rem(side_of[0] + side, 2) * span
        for first in range(0, span, 2 * size):
            lanes = pl.ds(pl.multiple_of(start + first, 128), 2 * size)
            out[:, lanes] = to_bf(to_f32(held[side, first : first + 2 * size, :]).T)


def gather_pieces(side, depth, pieces, shifts, after):
    rows, cols = pieces[0].shape[1:]
    count = 2 * len(pieces)
    return pl.pallas_call(
        functools.partial(gather_kernel, shifts),
        in_specs=[scalars] * 2 + [anywhere] * (1 + len(pieces)),
        out_specs=whole,
        out_shape=near((cols, count * rows), jnp.bfloat16),
        scratch_shapes=[
            pltpu.VMEM((2, len(pieces) * rows, cols), jnp.bfloat16),
            pltpu.SemaphoreType.DMA((count,)),
        ],
        compiler_params=params(),
        cost_estimate=cost(10**9, 4 * count * rows * cols),
    )(side, depth, after, *[to_far(piece) for piece in pieces])


def pass_kernel(*refs):
    pass


def pass_after(values, after):
    return pl.pallas_call(
        pass_kernel,
        in_specs=[anywhere] * (1 + len(after)),
        out_specs=anywhere,
        out_shape=shaped(values.shape, values.dtype),
        input_output_aliases={0: 0},
        compiler_params=params(),
        cost_estimate=cost(1, 1),
    )(values, *[to_far(array) for array in after])


def add_kernel(first, second, *rest):
    rest[-1][...] = to_bf(to_f32(first[...]) + to_f32(second[...]))


def add_after(first, second, after, held=()):
    outs = pl.pallas_call(
        add_kernel,
        in_specs=[whole, whole] + [anywhere] * (len(after) + len(held)),
        out_specs=[anywhere] * len(held) + [whole],
        out_shape=[far(array.shape, array.dtype) for array in held] + [near(first.shape, first.dtype)],
        input_output_aliases={2 + len(after) + place: place for place in range(len(held))},
        compiler_params=params(),
        cost_estimate=cost(first.size, 12 * first.size),
    )(to_near(first), second, *after, *[to_far(array) for array in held])
    return outs[-1], outs[:-1]


def shift(values, by):
    return lax.ppermute(values, "z", [(place, (place + by) % 8) for place in range(8)])


def swap(values, axis, size, bit):
    return lax.ppermute(values, axis, [(place, place ^ bit) for place in range(size)])


def shift(values, by):
    return lax.ppermute(values, "z", [(place, (place + by) % 8) for place in range(8)])


def local(pseudo_grad, error_buffer, basis_prev, master_weights, outer_momentum):
    core = lax.axis_index("core").astype(jnp.int32)
    rank = basis_prev.shape[1]
    grad, error = pseudo_grad[0], error_buffer[0]
    half = grad.shape[1] // 2
    which_mine, which_other = core.reshape(1), (1 - core).reshape(1)
    side = lax.axis_index("xh").astype(jnp.int32).reshape(1)
    depth = lax.axis_index("z").astype(jnp.int32).reshape(1)
    master, momentum = master_weights.T, outer_momentum.T

    given, merged_other, own = project(which_other, grad, error, basis_prev, jnp.bfloat16, master, momentum)
    received = swap(given, "core", 2, 1)
    across = swap(own, "xh", 2, 1)
    kept, merged_mine = project(which_mine, grad, error, basis_prev, jnp.float32)
    mine, bundle = combine(kept, received, own, across)
    up, down = shift(bundle, 1), shift(bundle, -1)
    up_two, down_two = shift(up, 1), shift(down, -1)
    chunks = lax.all_to_all(mine.reshape(16, rank // 16, half), plane, 0, 0, tiled=True)
    block = sum_chunks(chunks, (up, down))
    pieces = [bundle, up, down]
    block, _ = add_after(block, swap(block, "z", 8, 1), ())
    block, _ = add_after(block, swap(block, "z", 8, 2), (up_two, down_two))
    copies, (up, down) = spread(block, swap(block, "z", 8, 4), 16, (up_two, down_two))
    pieces += [up, down]
    up, down = shift(up, 1), shift(down, -1)
    far_side = shift(up, 1)
    pieces += [up, down, far_side]
    mine = lax.all_to_all(copies, plane, 0, 0, tiled=True)
    mine = pass_after(mine, (up, down)).reshape(rank, half)
    other = swap(mine, "core", 2, 1)

    before, _ = product_of(merged_mine, mine)
    (product, gram_mat), _ = product_of(merged_other, other, before)

    inverse = inverse_factor(gram_mat)
    product, _ = add_after(product, swap(product, "xh", 2, 1), (inverse, far_side))
    product, _ = add_after(product, swap(product, "z", 8, 1), ())
    basis_bf, basis_block = basis_of(which_mine, side, depth, inverse, mine, other, master.shape[0], product)
    product, _ = add_after(product, swap(product, "z", 8, 2), (basis_bf,))
    carried = gather_pieces(side, depth, pieces, (0, -1, 1, -2, 2, -3, 3, -4), product)
    arrived = swap(product, "z", 8, 4)

    error_next, weights_next, master_next, momentum_next = final(
        16, which_mine, inverse, product, arrived, basis_bf, merged_mine, merged_other, carried, basis_block,
        master, momentum,
    )
    return (error_next[None], weights_next, master_next.T, momentum_next.T)


def solution(mesh):
    fine = Mesh(mesh.devices.reshape(2, 8, 4, 2, 2), island + fsdp)
    in_specs = (
        P(island, fsdp, None),
        P(island, fsdp, None),
        P(fsdp, None),
        P(fsdp, island),
        P(fsdp, island),
    )
    out_specs = (
        P(island, fsdp, None),
        P(fsdp, None),
        P(fsdp, island),
        P(fsdp, island),
    )
    return jax.shard_map(local, mesh=fine, in_specs=in_specs, out_specs=out_specs, check_vma=False)
```

```python
import functools

import jax
import jax.numpy as jnp
from jax import lax
from jax.experimental import pallas as pl
from jax.experimental.pallas import tpu as pltpu
from jax.sharding import Mesh, PartitionSpec as P

momentum_coef = 0.9
outer_rate = 0.7
momentum_part = outer_rate * momentum_coef * momentum_coef
approx_part = outer_rate * (1.0 + momentum_coef)

island = ("xh", "z")
fsdp = ("y", "xl", "core")
plane = ("xh", "y", "xl")
panel = 32
group = 8
whole = pl.BlockSpec(memory_space=pltpu.VMEM)
anywhere = pl.BlockSpec(memory_space=pl.ANY)
scalars = pl.BlockSpec(memory_space=pltpu.SMEM)


def to_bf(values):
    return values.astype(jnp.bfloat16)


def to_f32(values):
    return values.astype(jnp.float32)


def times(left_mat, right_mat, left_dim=1, right_dim=0, precision=None):
    return lax.dot_general(
        left_mat,
        right_mat,
        (((left_dim,), (right_dim,)), ((), ())),
        precision=precision,
        preferred_element_type=jnp.float32,
    )


def shaped(shape, dtype):
    return jax.ShapeDtypeStruct(shape, dtype)


def far(shape, dtype):
    return pltpu.HBM(shape, dtype)


def near(shape, dtype):
    return pltpu.VMEM(shape, dtype)


def to_near(values):
    return pltpu.with_memory_space_constraint(values, pltpu.VMEM)


def to_far(values):
    return pltpu.with_memory_space_constraint(values, pltpu.HBM)


def params(size=16):
    return pltpu.CompilerParams(vmem_limit_bytes=size * 2**20)


def cost(flops, size):
    return pl.CostEstimate(flops=flops, bytes_accessed=size, transcendentals=0)


def fetch(source, target, sem):
    copy = pltpu.make_async_copy(source, target, sem)
    copy.start()
    return copy


def project_kernel(pieces, which, grad, error, basis, *rest):
    first = len(rest) > 6
    if first:
        master, momentum, left_out, merged_out, own_out, grads, errors, bases, sems, masters, momenta = rest
    else:
        left_out, merged_out, grads, errors, bases, sems = rest
    half = left_out.shape[1]
    width = half // pieces
    start = which[0] * half
    waits = [fetch(basis, bases, sems.at[0])]
    for piece in range(pieces):
        there = pl.ds(pl.multiple_of(start + piece * width, width), width)
        here = pl.ds(piece * width, width)
        waits.append(fetch(grad.at[:, there], grads.at[:, here], sems.at[1 + 2 * piece]))
        waits.append(fetch(error.at[:, there], errors.at[:, here], sems.at[2 + 2 * piece]))
    if first:
        waits.append(fetch(master, masters, sems.at[1 + 2 * pieces]))
        waits.append(fetch(momentum, momenta, sems.at[2 + 2 * pieces]))
    waits[0].wait()
    turned = to_bf(to_f32(bases[...]).T)
    for piece in range(pieces):
        here = slice(piece * width, (piece + 1) * width)
        waits[1 + 2 * piece].wait()
        waits[2 + 2 * piece].wait()
        merged = to_bf(to_f32(grads[:, here]) + to_f32(errors[:, here]))
        merged_out[:, here] = merged
        left_out[:, here] = times(turned, merged).astype(left_out.dtype)
    if first:
        waits[-2].wait()
        waits[-1].wait()
        own_out[...] = to_bf(masters[...] - momentum_part * momenta[...])


def project(which, grad, error, basis, dtype, master=None, momentum=None):
    rows, cols = grad.shape
    rank = basis.shape[1]
    half = cols // 2
    pieces = 5
    out_shape = [near((rank, half), dtype), near((rows, half), jnp.bfloat16)]
    operands = [which, to_far(grad), to_far(error), to_far(basis)]
    scratch = [
        pltpu.VMEM((rows, half), jnp.bfloat16),
        pltpu.VMEM((rows, half), jnp.bfloat16),
        pltpu.VMEM((rows, rank), jnp.bfloat16),
        pltpu.SemaphoreType.DMA((3 + 2 * pieces,)),
    ]
    if master is not None:
        operands += [to_far(master), to_far(momentum)]
        out_shape.append(near(master.shape, jnp.bfloat16))
        scratch += [pltpu.VMEM(master.shape, jnp.float32)] * 2
    return pl.pallas_call(
        functools.partial(project_kernel, pieces),
        in_specs=[scalars] + [anywhere] * (len(operands) - 1),
        out_specs=[whole] * len(out_shape),
        out_shape=out_shape,
        scratch_shapes=scratch,
        compiler_params=params(24),
        cost_estimate=cost(rows * cols * rank, 2 * rows * cols),
    )(*operands)


def combine_kernel(kept, received, mine_out):
    mine_out[...] = to_bf(kept[...] + to_f32(received[...]))


def combine(kept, received):
    return pl.pallas_call(
        combine_kernel,
        in_specs=[whole] * 2,
        out_specs=whole,
        out_shape=shaped(kept.shape, jnp.bfloat16),
        compiler_params=params(),
        cost_estimate=cost(kept.size, 8 * kept.size),
    )(to_near(kept), to_near(received))


def bundle_kernel(own, across, out):
    out[0] = own[...]
    out[1] = across[...]


def bundle_of(own, across):
    return pl.pallas_call(
        bundle_kernel,
        in_specs=[whole] * 2,
        out_specs=whole,
        out_shape=far((2,) + own.shape, own.dtype),
        compiler_params=params(),
        cost_estimate=cost(10**11, own.size),
    )(to_near(own), to_near(across))


def sum_kernel(chunks, *rest):
    out = rest[-1]
    total = to_f32(chunks[0])
    for place in range(1, chunks.shape[0]):
        total = total + to_f32(chunks[place])
    out[...] = to_bf(total)


def sum_chunks(chunks, after):
    return pl.pallas_call(
        sum_kernel,
        in_specs=[whole] + [anywhere] * len(after),
        out_specs=whole,
        out_shape=near(chunks.shape[1:], jnp.bfloat16),
        compiler_params=params(),
        cost_estimate=cost(chunks.size, 2 * chunks.size),
    )(to_near(chunks), *[to_far(array) for array in after])


def sum_pairs(own, opposite, before, after):
    return (to_f32(own[...]) + to_f32(opposite[...])) + (to_f32(before[...]) + to_f32(after[...]))


def spread_kernel(count, block, opposite, before, after, *rest):
    out = rest[-1]
    total = to_bf(sum_pairs(block, opposite, before, after))
    for place in range(count):
        out[place] = total


def spread(block, arrived, count, held):
    outs = pl.pallas_call(
        functools.partial(spread_kernel, count),
        in_specs=[whole] * 4 + [anywhere] * len(held),
        out_specs=[anywhere] * len(held) + [whole],
        out_shape=[far(array.shape, array.dtype) for array in held]
        + [far((count,) + block.shape, jnp.bfloat16)],
        input_output_aliases={4 + place: place for place in range(len(held))},
        compiler_params=params(),
        cost_estimate=cost(block.size, 2 * count * block.size),
    )(*[to_near(array) for array in (block, *arrived)], *[to_far(array) for array in held])
    return outs[-1], outs[:-1]


def product_kernel(first, merged, left, *rest):
    values = left[...]
    product = times(merged[...], values, 1, 1)
    gram_mat = times(values, values, 1, 1)
    product_out, gram_out = rest[-2:]
    if not first:
        product = rest[0][...] + product
        gram_mat = rest[1][...] + gram_mat
    product_out[...] = product.astype(product_out.dtype)
    gram_out[...] = gram_mat


def product_of(merged, left, before=(), held=()):
    rows = merged.shape[0]
    rank = left.shape[0]
    outs = pl.pallas_call(
        functools.partial(product_kernel, not before),
        in_specs=[whole] * (2 + len(before)) + [anywhere] * len(held),
        out_specs=[anywhere] * len(held) + [whole] * 2,
        out_shape=[far(array.shape, array.dtype) for array in held]
        + [near((rows, rank), jnp.bfloat16 if before else jnp.float32), near((rank, rank), jnp.float32)],
        input_output_aliases={2 + len(before) + place: place for place in range(len(held))},
        compiler_params=params(),
        cost_estimate=cost(2 * rows * left.size, 4 * left.size),
    )(to_near(merged), to_near(left), *[to_near(array) for array in before], *[to_far(array) for array in held])
    return outs[-2:], outs[:-2]


def factor_kernel(gram_mat, *refs):
    inverse_out, state, below_all = refs[-3:]
    rank = gram_mat.shape[0]
    exact = lax.Precision.HIGHEST
    row_of = lax.broadcasted_iota(jnp.int32, (rank, rank), 0)
    col_of = lax.broadcasted_iota(jnp.int32, (rank, rank), 1)
    state[...] = gram_mat[...]
    below_all[...] = jnp.where(row_of == col_of, 1.0, 0.0)
    row_of, col_of = row_of[:panel], col_of[:panel]
    for start in range(0, rank, panel):
        stop = start + panel
        rows, below = state[start:stop, :], below_all[start:stop, :]
        for first in range(0, panel, group):
            columns = [
                jnp.broadcast_to(rows[:, start + k : start + k + 1], (panel, rank))
                for k in range(first, first + group)
            ]
            for place in range(group):
                k = first + place
                factor = jnp.where(row_of > k, columns[place], 0.0) * (1.0 / columns[place][k : k + 1, :])
                for later in range(place + 1, group):
                    columns[later] = columns[later] - factor * columns[later][k : k + 1, :]
                rows = rows - factor * rows[k : k + 1, :]
                below = below - factor * below[k : k + 1, :]
        diagonal = jnp.sum(jnp.where(col_of == row_of + start, rows, 0.0), axis=1, keepdims=True)
        scale = lax.rsqrt(diagonal)
        rows, below = rows * scale, below * scale
        inverse_out[start:stop, :] = below
        if stop < rank:
            later = rows.T[stop:, :]
            state[stop:, :] -= times(later, rows, precision=exact)
            below_all[stop:, :] -= times(later, below, precision=exact)


def inverse_factor(gram_mat, kept):
    rank = gram_mat.shape[0]
    return pl.pallas_call(
        factor_kernel,
        in_specs=[whole] + [anywhere] * len(kept),
        out_specs=whole,
        out_shape=near((rank, rank), jnp.float32),
        scratch_shapes=[pltpu.VMEM((rank, rank), jnp.float32)] * 2,
        compiler_params=params(),
        cost_estimate=cost(10**9, 4 * rank * rank * 4),
    )(to_near(gram_mat), *[to_near(array) for array in kept])


def basis_kernel(which, side, depth, inverse, mine, other, _, out, block_out, held):
    half = mine.shape[1]
    value = inverse[...]
    high = to_bf(value)
    low = to_bf(value - to_f32(high))

    def put(left, start):
        left = left[...]
        basis = times(high, left) + times(low, left)
        out[:, pl.ds(pl.multiple_of(start, half), half)] = to_bf(basis)

    put(mine, which[0] * half)
    put(other, (1 - which[0]) * half)
    size = block_out.shape[0]
    pair = side[0] * half + (depth[0] // 2) * (2 * size)
    held[...] = to_f32(out[:, pl.ds(pl.multiple_of(pair, 2 * size), 2 * size)]).T
    block_out[...] = to_bf(held[pl.ds(pl.multiple_of(lax.rem(depth[0], 2) * size, size), size), :])


def basis_of(which, side, depth, inverse, mine, other, size, after):
    rank, half = mine.shape
    return pl.pallas_call(
        basis_kernel,
        in_specs=[scalars] * 3 + [whole] * 3 + [anywhere],
        out_specs=[whole] * 2,
        out_shape=[near((rank, 2 * half), jnp.bfloat16), near((size, rank), jnp.bfloat16)],
        scratch_shapes=[pltpu.VMEM((2 * size, rank), jnp.float32)],
        compiler_params=params(),
        cost_estimate=cost(8 * rank * rank * half, 8 * rank * half),
    )(which, side, depth, to_near(inverse), to_near(mine), to_near(other), after)


def final_kernel(
    islands, pieces, which, inverse, product, opposite, before, after, basis, merged_mine, merged_other, carried, block, master,
    momentum, error_out, weights_out, master_out, momentum_out, errors, weights, masters, momenta, sems,
):
    total = sum_pairs(product, opposite, before, after)
    q_avg = to_bf(times(total, inverse[...], 1, 1, lax.Precision.HIGHEST) / islands)
    half = merged_mine.shape[1]
    width = half // pieces
    waits = []
    for number, merged in enumerate((merged_mine, merged_other)):
        start = lax.rem(which[0] + number, 2) * half
        for piece in range(pieces):
            lanes = pl.ds(pl.multiple_of(start + piece * width, width), width)
            approx = times(q_avg, basis[:, lanes])
            errors[:, lanes] = to_bf(to_f32(merged[:, piece * width : (piece + 1) * width]) - approx)
            waits.append(fetch(errors.at[:, lanes], error_out.at[:, lanes], sems.at[len(waits)]))
            weights[:, lanes] = to_bf(to_f32(carried[:, lanes]) - approx_part * approx)
            waits.append(fetch(weights.at[:, lanes], weights_out.at[:, lanes], sems.at[len(waits)]))
    update = times(block[...], q_avg, 1, 1)
    momentum_next = momentum_coef * momentum[...] + update
    momenta[...] = momentum_next
    waits.append(fetch(momenta, momentum_out, sems.at[len(waits)]))
    masters[...] = master[...] - outer_rate * (update + momentum_coef * momentum_next)
    waits.append(fetch(masters, master_out, sems.at[len(waits)]))
    for copy in waits:
        copy.wait()


def final(islands, which, inverse, product, arrived, basis, mine, other, carried, block, master, momentum):
    rows, half = mine.shape
    rank = basis.shape[0]
    cols = 2 * half
    own = master.shape
    pieces = 5
    return pl.pallas_call(
        functools.partial(final_kernel, islands, pieces),
        in_specs=[scalars] + [whole] * 12,
        out_specs=[anywhere] * 4,
        out_shape=[
            shaped((rows, cols), jnp.bfloat16),
            shaped((rows, cols), jnp.bfloat16),
            shaped(own, jnp.float32),
            shaped(own, jnp.float32),
        ],
        scratch_shapes=[pltpu.VMEM((rows, cols), jnp.bfloat16)] * 2
        + [pltpu.VMEM(own, jnp.float32)] * 2
        + [pltpu.SemaphoreType.DMA((4 * pieces + 2,))],
        compiler_params=params(24),
        cost_estimate=cost(2 * rows * cols * rank, 8 * rows * cols),
    )(
        which, to_near(inverse), *[to_near(array) for array in (product, *arrived)], to_near(basis), to_near(mine), to_near(other),
        to_near(carried), to_near(block), master, momentum,
    )


def gather_kernel(shifts, side_of, depth, _, *refs):
    pieces, out, held, sems = refs[:-3], refs[-3], refs[-2], refs[-1]
    size = pieces[0].shape[1]
    count = len(shifts)
    waits = []
    for number in range(count):
        z_of = lax.rem(depth[0] + (shifts[number] + count), count)
        rows = pl.ds(pl.multiple_of(z_of * size, size), size)
        for side in range(2):
            waits.append(fetch(pieces[number].at[side], held.at[side, rows], sems.at[len(waits)]))
    for copy in waits:
        copy.wait()
    span = count * size
    for side in range(2):
        start = lax.rem(side_of[0] + side, 2) * span
        for first in range(0, span, 2 * size):
            lanes = pl.ds(pl.multiple_of(start + first, 128), 2 * size)
            out[:, lanes] = to_bf(to_f32(held[side, first : first + 2 * size, :]).T)


def gather_pieces(side, depth, pieces, shifts, after):
    rows, cols = pieces[0].shape[1:]
    count = 2 * len(pieces)
    return pl.pallas_call(
        functools.partial(gather_kernel, shifts),
        in_specs=[scalars] * 2 + [anywhere] * (1 + len(pieces)),
        out_specs=whole,
        out_shape=near((cols, count * rows), jnp.bfloat16),
        scratch_shapes=[
            pltpu.VMEM((2, len(pieces) * rows, cols), jnp.bfloat16),
            pltpu.SemaphoreType.DMA((count,)),
        ],
        compiler_params=params(),
        cost_estimate=cost(10**9, 4 * count * rows * cols),
    )(side, depth, after, *[to_far(piece) for piece in pieces])


def pass_kernel(*refs):
    pass


def pass_after(values, after):
    return pl.pallas_call(
        pass_kernel,
        in_specs=[anywhere] * (1 + len(after)),
        out_specs=anywhere,
        out_shape=shaped(values.shape, values.dtype),
        input_output_aliases={0: 0},
        compiler_params=params(),
        cost_estimate=cost(1, 1),
    )(values, *[to_far(array) for array in after])


def add_kernel(first, second, *rest):
    rest[-1][...] = to_bf(to_f32(first[...]) + to_f32(second[...]))


def add_after(first, second, after, held=()):
    outs = pl.pallas_call(
        add_kernel,
        in_specs=[whole, whole] + [anywhere] * (len(after) + len(held)),
        out_specs=[anywhere] * len(held) + [whole],
        out_shape=[far(array.shape, array.dtype) for array in held] + [near(first.shape, first.dtype)],
        input_output_aliases={2 + len(after) + place: place for place in range(len(held))},
        compiler_params=params(),
        cost_estimate=cost(first.size, 12 * first.size),
    )(to_near(first), to_near(second), *after, *[to_far(array) for array in held])
    return outs[-1], outs[:-1]


def from_pairs(values):
    evens, odds = range(0, 8, 2), range(1, 8, 2)

    def send(even_by, odd_by):
        routes = [(place, (place + even_by) % 8) for place in evens]
        return lax.ppermute(values, "z", routes + [(place, (place + odd_by) % 8) for place in odds])

    return send(-3, 3), send(-1, 1), send(-2, 2)


def shift(values, by):
    return lax.ppermute(values, "z", [(place, (place + by) % 8) for place in range(8)])


def swap(values, axis, size, bit):
    return lax.ppermute(values, axis, [(place, place ^ bit) for place in range(size)])


def shift(values, by):
    return lax.ppermute(values, "z", [(place, (place + by) % 8) for place in range(8)])


def local(pseudo_grad, error_buffer, basis_prev, master_weights, outer_momentum):
    core = lax.axis_index("core").astype(jnp.int32)
    rank = basis_prev.shape[1]
    grad, error = pseudo_grad[0], error_buffer[0]
    half = grad.shape[1] // 2
    which_mine, which_other = core.reshape(1), (1 - core).reshape(1)
    side = lax.axis_index("xh").astype(jnp.int32).reshape(1)
    depth = lax.axis_index("z").astype(jnp.int32).reshape(1)
    master, momentum = master_weights.T, outer_momentum.T

    given, merged_other, own = project(which_other, grad, error, basis_prev, jnp.bfloat16, master, momentum)
    received = swap(given, "core", 2, 1)
    across = swap(own, "xh", 2, 1)
    kept, merged_mine = project(which_mine, grad, error, basis_prev, jnp.float32)
    mine = combine(kept, received)
    bundle = bundle_of(own, across)
    up, down = shift(bundle, 1), shift(bundle, -1)
    up_two, down_two = shift(up, 1), shift(down, -1)
    chunks = lax.all_to_all(mine.reshape(16, rank // 16, half), plane, 0, 0, tiled=True)
    block = sum_chunks(chunks, (up, down))
    pieces = [bundle, up, down]
    block, _ = add_after(block, swap(block, "z", 8, 1), ())
    copies, (up, down) = spread(block, from_pairs(block), 16, (up_two, down_two))
    pieces += [up, down]
    up, down = shift(up, 1), shift(down, -1)
    mine = lax.all_to_all(copies, plane, 0, 0, tiled=True)
    mine = pass_after(mine, (up, down)).reshape(rank, half)
    other = swap(mine, "core", 2, 1)

    before, _ = product_of(merged_mine, mine)
    (product, gram_mat), (up,) = product_of(merged_other, other, before, (up,))
    far_side = shift(up, 1)
    pieces += [up, down, far_side]

    inverse = inverse_factor(gram_mat, (mine, other))
    product, _ = add_after(product, swap(product, "xh", 2, 1), (inverse,))
    basis_bf, basis_block = basis_of(which_mine, side, depth, inverse, mine, other, master.shape[0], product)
    product, _ = add_after(product, swap(product, "z", 8, 1), (basis_bf, far_side))
    carried = gather_pieces(side, depth, pieces, (0, -1, 1, -2, 2, -3, 3, -4), product)
    arrived = from_pairs(product)

    error_next, weights_next, master_next, momentum_next = final(
        16, which_mine, inverse, product, arrived, basis_bf, merged_mine, merged_other, carried, basis_block,
        master, momentum,
    )
    return (error_next[None], weights_next, master_next.T, momentum_next.T)


def solution(mesh):
    fine = Mesh(mesh.devices.reshape(2, 8, 4, 2, 2), island + fsdp)
    in_specs = (
        P(island, fsdp, None),
        P(island, fsdp, None),
        P(fsdp, None),
        P(fsdp, island),
        P(fsdp, island),
    )
    out_specs = (
        P(island, fsdp, None),
        P(fsdp, None),
        P(fsdp, island),
        P(fsdp, island),
    )
    return jax.shard_map(local, mesh=fine, in_specs=in_specs, out_specs=out_specs, check_vma=False)
```

```python
import functools

import jax
import jax.numpy as jnp
from jax import lax
from jax.experimental import pallas as pl
from jax.experimental.pallas import tpu as pltpu
from jax.sharding import Mesh, PartitionSpec as P

momentum_coef = 0.9
outer_rate = 0.7
momentum_part = outer_rate * momentum_coef * momentum_coef
approx_part = outer_rate * (1.0 + momentum_coef)

island = ("xh", "z")
fsdp = ("y", "xl", "core")
plane = ("xh", "y", "xl")
panel = 32
group = 16
whole = pl.BlockSpec(memory_space=pltpu.VMEM)
anywhere = pl.BlockSpec(memory_space=pl.ANY)
scalars = pl.BlockSpec(memory_space=pltpu.SMEM)


def to_bf(values):
    return values.astype(jnp.bfloat16)


def to_f32(values):
    return values.astype(jnp.float32)


def times(left_mat, right_mat, left_dim=1, right_dim=0, precision=None):
    return lax.dot_general(
        left_mat,
        right_mat,
        (((left_dim,), (right_dim,)), ((), ())),
        precision=precision,
        preferred_element_type=jnp.float32,
    )


def shaped(shape, dtype):
    return jax.ShapeDtypeStruct(shape, dtype)


def far(shape, dtype):
    return pltpu.HBM(shape, dtype)


def all_near(arrays):
    return [to_near(array) for array in arrays]


def near(shape, dtype):
    return pltpu.VMEM(shape, dtype)


def to_near(values):
    return pltpu.with_memory_space_constraint(values, pltpu.VMEM)


def to_far(values):
    return pltpu.with_memory_space_constraint(values, pltpu.HBM)


def params(size=16):
    return pltpu.CompilerParams(vmem_limit_bytes=size * 2**20)


def cost(flops, size):
    return pl.CostEstimate(flops=flops, bytes_accessed=size, transcendentals=0)


def fetch(source, target, sem):
    copy = pltpu.make_async_copy(source, target, sem)
    copy.start()
    return copy


def project_kernel(pieces, which, grad, error, basis, *rest):
    first = len(rest) > 7
    if first:
        master, momentum, left_out, merged_out, own_out, grads, errors, bases, sems, masters, momenta = rest
    else:
        left_out, merged_out, grads, errors, bases, sems = rest[-6:]
    half = left_out.shape[1]
    width = half // pieces
    start = which[0] * half
    waits = [fetch(basis, bases, sems.at[0])]
    for piece in range(pieces):
        there = pl.ds(pl.multiple_of(start + piece * width, width), width)
        here = pl.ds(piece * width, width)
        waits.append(fetch(grad.at[:, there], grads.at[:, here], sems.at[1 + 2 * piece]))
        waits.append(fetch(error.at[:, there], errors.at[:, here], sems.at[2 + 2 * piece]))
    if first:
        waits.append(fetch(master, masters, sems.at[1 + 2 * pieces]))
        waits.append(fetch(momentum, momenta, sems.at[2 + 2 * pieces]))
    waits[0].wait()
    turned = to_bf(to_f32(bases[...]).T)
    for piece in range(pieces):
        here = slice(piece * width, (piece + 1) * width)
        waits[1 + 2 * piece].wait()
        waits[2 + 2 * piece].wait()
        merged = to_bf(to_f32(grads[:, here]) + to_f32(errors[:, here]))
        merged_out[:, here] = merged
        left_out[:, here] = times(turned, merged).astype(left_out.dtype)
    if first:
        waits[-2].wait()
        waits[-1].wait()
        own_out[...] = to_bf(masters[...] - momentum_part * momenta[...])


def project(which, grad, error, basis, dtype, master=None, momentum=None, held=()):
    rows, cols = grad.shape
    rank = basis.shape[1]
    half = cols // 2
    pieces = 5
    out_shape = [near((rank, half), dtype), near((rows, half), jnp.bfloat16)]
    operands = [which, to_far(grad), to_far(error), to_far(basis)]
    scratch = [
        pltpu.VMEM((rows, half), jnp.bfloat16),
        pltpu.VMEM((rows, half), jnp.bfloat16),
        pltpu.VMEM((rows, rank), jnp.bfloat16),
        pltpu.SemaphoreType.DMA((3 + 2 * pieces,)),
    ]
    operands += all_near(held)
    if master is not None:
        operands += [to_far(master), to_far(momentum)]
        out_shape.append(near(master.shape, jnp.bfloat16))
        scratch += [pltpu.VMEM(master.shape, jnp.float32)] * 2
    return pl.pallas_call(
        functools.partial(project_kernel, pieces),
        in_specs=[scalars] + [anywhere] * (len(operands) - 1),
        out_specs=[whole] * len(out_shape),
        out_shape=out_shape,
        scratch_shapes=scratch,
        compiler_params=params(24),
        cost_estimate=cost(rows * cols * rank, 2 * rows * cols),
    )(*operands)


def combine_kernel(kept, received, *rest):
    rest[-1][...] = to_bf(kept[...] + to_f32(received[...]))


def combine(kept, received, held):
    return pl.pallas_call(
        combine_kernel,
        in_specs=[whole] * 2 + [anywhere] * len(held),
        out_specs=whole,
        out_shape=shaped(kept.shape, jnp.bfloat16),
        compiler_params=params(),
        cost_estimate=cost(kept.size, 8 * kept.size),
    )(to_near(kept), to_near(received), *all_near(held))


def bundle_kernel(own, across, out):
    out[0] = own[...]
    out[1] = across[...]


def bundle_of(own, across):
    return pl.pallas_call(
        bundle_kernel,
        in_specs=[whole] * 2,
        out_specs=whole,
        out_shape=far((2,) + own.shape, own.dtype),
        compiler_params=params(),
        cost_estimate=cost(10**11, own.size),
    )(to_near(own), to_near(across))


def sum_kernel(chunks, *rest):
    out = rest[-1]
    total = to_f32(chunks[0])
    for place in range(1, chunks.shape[0]):
        total = total + to_f32(chunks[place])
    out[...] = to_bf(total)


def sum_chunks(chunks, after, held):
    return pl.pallas_call(
        sum_kernel,
        in_specs=[whole] + [anywhere] * (len(after) + len(held)),
        out_specs=whole,
        out_shape=near(chunks.shape[1:], jnp.bfloat16),
        compiler_params=params(),
        cost_estimate=cost(chunks.size, 2 * chunks.size),
    )(to_near(chunks), *[to_far(array) for array in after], *all_near(held))


def sum_pairs(own, opposite, before, after):
    return (to_f32(own[...]) + to_f32(opposite[...])) + (to_f32(before[...]) + to_f32(after[...]))


def spread_kernel(count, block, before, after, opposite, *rest):
    out = rest[-1]
    total = to_bf(sum_pairs(block, opposite, before, after))
    for place in range(count):
        out[place] = total


def spread(block, arrived, count, held):
    outs = pl.pallas_call(
        functools.partial(spread_kernel, count),
        in_specs=[whole] * 4 + [anywhere] * len(held),
        out_specs=[anywhere] * len(held) + [whole],
        out_shape=[far(array.shape, array.dtype) for array in held]
        + [far((count,) + block.shape, jnp.bfloat16)],
        input_output_aliases={4 + place: place for place in range(len(held))},
        compiler_params=params(),
        cost_estimate=cost(block.size, 2 * count * block.size),
    )(*[to_near(array) for array in (block, *arrived)], *[to_far(array) for array in held])
    return outs[-1], outs[:-1]


def product_kernel(first, merged, left, *rest):
    values = left[...]
    product = times(merged[...], values, 1, 1)
    gram_mat = times(values, values, 1, 1)
    product_out, gram_out = rest[-2:]
    if not first:
        product = rest[0][...] + product
        gram_mat = rest[1][...] + gram_mat
    product_out[...] = product.astype(product_out.dtype)
    gram_out[...] = gram_mat


def product_of(merged, left, before=(), held=()):
    rows = merged.shape[0]
    rank = left.shape[0]
    outs = pl.pallas_call(
        functools.partial(product_kernel, not before),
        in_specs=[whole] * (2 + len(before)) + [anywhere] * len(held),
        out_specs=[anywhere] * len(held) + [whole] * 2,
        out_shape=[far(array.shape, array.dtype) for array in held]
        + [near((rows, rank), jnp.bfloat16 if before else jnp.float32), near((rank, rank), jnp.float32)],
        input_output_aliases={2 + len(before) + place: place for place in range(len(held))},
        compiler_params=params(),
        cost_estimate=cost(2 * rows * left.size, 4 * left.size),
    )(to_near(merged), to_near(left), *[to_near(array) for array in before], *[to_far(array) for array in held])
    return outs[-2:], outs[:-2]


def factor_kernel(gram_mat, *refs):
    inverse_out, state, below_all = refs[-3:]
    rank = gram_mat.shape[0]
    exact = lax.Precision.HIGHEST
    row_of = lax.broadcasted_iota(jnp.int32, (rank, rank), 0)
    col_of = lax.broadcasted_iota(jnp.int32, (rank, rank), 1)
    state[...] = gram_mat[...]
    below_all[...] = jnp.where(row_of == col_of, 1.0, 0.0)
    row_of, col_of = row_of[:panel], col_of[:panel]
    for start in range(0, rank, panel):
        stop = start + panel
        rows, below = state[start:stop, :], below_all[start:stop, :]
        for first in range(0, panel, group):
            columns = [
                jnp.broadcast_to(rows[:, start + k : start + k + 1], (panel, rank))
                for k in range(first, first + group)
            ]
            for place in range(group):
                k = first + place
                factor = jnp.where(row_of > k, columns[place], 0.0) * (1.0 / columns[place][k : k + 1, :])
                for later in range(place + 1, group):
                    columns[later] = columns[later] - factor * columns[later][k : k + 1, :]
                rows = rows - factor * rows[k : k + 1, :]
                below = below - factor * below[k : k + 1, :]
        diagonal = jnp.sum(jnp.where(col_of == row_of + start, rows, 0.0), axis=1, keepdims=True)
        scale = lax.rsqrt(diagonal)
        rows, below = rows * scale, below * scale
        inverse_out[start:stop, :] = below
        if stop < rank:
            later = rows.T[stop:, :]
            state[stop:, :] -= times(later, rows, precision=exact)
            below_all[stop:, :] -= times(later, below, precision=exact)


def inverse_factor(gram_mat, kept):
    rank = gram_mat.shape[0]
    return pl.pallas_call(
        factor_kernel,
        in_specs=[whole] + [anywhere] * len(kept),
        out_specs=whole,
        out_shape=near((rank, rank), jnp.float32),
        scratch_shapes=[pltpu.VMEM((rank, rank), jnp.float32)] * 2,
        compiler_params=params(),
        cost_estimate=cost(10**9, 4 * rank * rank * 4),
    )(to_near(gram_mat), *[to_near(array) for array in kept])


def basis_kernel(which, side, depth, inverse, mine, other, _, out, block_out, held):
    half = mine.shape[1]
    value = inverse[...]
    high = to_bf(value)
    low = to_bf(value - to_f32(high))

    def put(left, start):
        left = left[...]
        basis = times(high, left) + times(low, left)
        out[:, pl.ds(pl.multiple_of(start, half), half)] = to_bf(basis)

    put(mine, which[0] * half)
    put(other, (1 - which[0]) * half)
    size = block_out.shape[0]
    pair = side[0] * half + (depth[0] // 2) * (2 * size)
    held[...] = to_f32(out[:, pl.ds(pl.multiple_of(pair, 2 * size), 2 * size)]).T
    block_out[...] = to_bf(held[pl.ds(pl.multiple_of(lax.rem(depth[0], 2) * size, size), size), :])


def basis_of(which, side, depth, inverse, mine, other, size, after):
    rank, half = mine.shape
    return pl.pallas_call(
        basis_kernel,
        in_specs=[scalars] * 3 + [whole] * 3 + [anywhere],
        out_specs=[whole] * 2,
        out_shape=[near((rank, 2 * half), jnp.bfloat16), near((size, rank), jnp.bfloat16)],
        scratch_shapes=[pltpu.VMEM((2 * size, rank), jnp.float32)],
        compiler_params=params(),
        cost_estimate=cost(8 * rank * rank * half, 8 * rank * half),
    )(which, side, depth, to_near(inverse), to_near(mine), to_near(other), after)


def final_kernel(
    islands, pieces, which, inverse, product, before, after, opposite, basis, merged_mine, merged_other, carried, block, master,
    momentum, error_out, weights_out, master_out, momentum_out, errors, weights, masters, momenta, sems,
):
    total = sum_pairs(product, opposite, before, after)
    q_avg = to_bf(times(total, inverse[...], 1, 1, lax.Precision.HIGHEST) / islands)
    half = merged_mine.shape[1]
    width = half // pieces
    waits = []
    for number, merged in enumerate((merged_mine, merged_other)):
        start = lax.rem(which[0] + number, 2) * half
        for piece in range(pieces):
            lanes = pl.ds(pl.multiple_of(start + piece * width, width), width)
            approx = times(q_avg, basis[:, lanes])
            errors[:, lanes] = to_bf(to_f32(merged[:, piece * width : (piece + 1) * width]) - approx)
            waits.append(fetch(errors.at[:, lanes], error_out.at[:, lanes], sems.at[len(waits)]))
            weights[:, lanes] = to_bf(to_f32(carried[:, lanes]) - approx_part * approx)
            waits.append(fetch(weights.at[:, lanes], weights_out.at[:, lanes], sems.at[len(waits)]))
    update = times(block[...], q_avg, 1, 1)
    momentum_next = momentum_coef * momentum[...] + update
    momenta[...] = momentum_next
    waits.append(fetch(momenta, momentum_out, sems.at[len(waits)]))
    masters[...] = master[...] - outer_rate * (update + momentum_coef * momentum_next)
    waits.append(fetch(masters, master_out, sems.at[len(waits)]))
    for copy in waits:
        copy.wait()


def final(islands, which, inverse, product, arrived, basis, mine, other, carried, block, master, momentum):
    rows, half = mine.shape
    rank = basis.shape[0]
    cols = 2 * half
    own = master.shape
    pieces = 5
    return pl.pallas_call(
        functools.partial(final_kernel, islands, pieces),
        in_specs=[scalars] + [whole] * 12,
        out_specs=[anywhere] * 4,
        out_shape=[
            shaped((rows, cols), jnp.bfloat16),
            shaped((rows, cols), jnp.bfloat16),
            shaped(own, jnp.float32),
            shaped(own, jnp.float32),
        ],
        scratch_shapes=[pltpu.VMEM((rows, cols), jnp.bfloat16)] * 2
        + [pltpu.VMEM(own, jnp.float32)] * 2
        + [pltpu.SemaphoreType.DMA((4 * pieces + 2,))],
        compiler_params=params(24),
        cost_estimate=cost(2 * rows * cols * rank, 8 * rows * cols),
    )(
        which, to_near(inverse), *[to_near(array) for array in (product, *arrived)], to_near(basis), to_near(mine), to_near(other),
        to_near(carried), to_near(block), master, momentum,
    )


def gather_kernel(shifts, side_of, depth, *refs):
    count = len(shifts)
    pieces, out, token, held, sems = refs[:count], *refs[-4:]
    token[...] = jnp.zeros_like(token)
    size = pieces[0].shape[1]
    ring = held.shape[1] // size
    waits = []
    for number in range(count):
        z_of = lax.rem(depth[0] + (shifts[number] + ring), ring)
        rows = pl.ds(pl.multiple_of(z_of * size, size), size)
        for half in range(2):
            waits.append(fetch(pieces[number].at[half], held.at[half, rows], sems.at[len(waits)]))
    for copy in waits:
        copy.wait()
    pairs = ring // 2
    own = depth[0] // 2
    beyond = own + lax.rem(depth[0], 2) * 2 + (pairs - 1)
    turn = 0 if len(refs) == count + 4 else 2
    span = ring * size
    for pair in (own, beyond):
        first = lax.rem(pair + turn, pairs) * (2 * size)
        for half in range(2):
            start = lax.rem(side_of[0] + half, 2) * span
            lanes = pl.ds(pl.multiple_of(start + first, 2 * size), 2 * size)
            rows = pl.ds(pl.multiple_of(first, 2 * size), 2 * size)
            out[:, lanes] = to_bf(to_f32(held[half, rows, :]).T)


def gather_pieces(side, depth, pieces, shifts, before=()):
    rows, cols = pieces[0].shape[1:]
    count = len(pieces)
    ring = 8
    return pl.pallas_call(
        functools.partial(gather_kernel, shifts),
        in_specs=[scalars] * 2 + [anywhere] * count + ([whole, anywhere] if before else []),
        out_specs=[whole] * 2,
        out_shape=[near((cols, 2 * ring * rows), jnp.bfloat16), near((8, 128), jnp.float32)],
        scratch_shapes=[
            pltpu.VMEM((2, ring * rows, cols), jnp.bfloat16),
            pltpu.SemaphoreType.DMA((2 * count,)),
        ],
        input_output_aliases={2 + count: 0} if before else {},
        compiler_params=params(),
        cost_estimate=cost(10**9, 4 * count * rows * cols),
    )(side, depth, *pieces, *all_near(before))


def pass_kernel(*refs):
    pass


def pass_through(arrays):
    return pl.pallas_call(
        pass_kernel,
        in_specs=[anywhere] * len(arrays),
        out_specs=[anywhere] * len(arrays),
        out_shape=[far(array.shape, array.dtype) for array in arrays],
        input_output_aliases={place: place for place in range(len(arrays))},
        compiler_params=params(),
        cost_estimate=cost(10**11, 1),
    )(*[to_far(array) for array in arrays])


def pass_after(values, after):
    return pl.pallas_call(
        pass_kernel,
        in_specs=[anywhere] * (len(after) + len(after[-1])),
        out_specs=anywhere,
        out_shape=shaped(values.shape, values.dtype),
        input_output_aliases={0: 0},
        compiler_params=params(),
        cost_estimate=cost(1, 1),
    )(values, *after[:-1], *all_near(after[-1]))


def add_kernel(first, second, *rest):
    rest[-1][...] = to_bf(to_f32(first[...]) + to_f32(second[...]))


def add_after(first, second, after, held=()):
    outs = pl.pallas_call(
        add_kernel,
        in_specs=[whole, whole] + [anywhere] * (len(after) + len(held)),
        out_specs=[anywhere] * len(held) + [whole],
        out_shape=[far(array.shape, array.dtype) for array in held] + [near(first.shape, first.dtype)],
        input_output_aliases={2 + len(after) + place: place for place in range(len(held))},
        compiler_params=params(),
        cost_estimate=cost(first.size, 12 * first.size),
    )(to_near(first), to_near(second), *after, *[to_far(array) for array in held])
    return outs[-1], outs[:-1]


def from_pairs(values):
    evens, odds = range(0, 8, 2), range(1, 8, 2)

    def send(even_by, odd_by):
        routes = [(place, (place + even_by) % 8) for place in evens]
        return lax.ppermute(values, "z", routes + [(place, (place + odd_by) % 8) for place in odds])

    before = send(-1, 1)
    after = send(-2, 2)
    return before, after, send(-3, 3)


def from_quad(values):
    def send(mask):
        return lax.ppermute(values, island, [(place, place ^ mask) for place in range(16)])

    beside = send(1)
    across = send(8)
    return beside, across, send(9)


def add_quad_kernel(own, beside, across, corner, *rest):
    rest[-1][...] = to_bf(sum_pairs(own, across, beside, corner))


def add_quad(own, arrived, after):
    return pl.pallas_call(
        add_quad_kernel,
        in_specs=[whole] * 4 + [anywhere] * len(after),
        out_specs=whole,
        out_shape=near(own.shape, own.dtype),
        compiler_params=params(),
        cost_estimate=cost(own.size, 12 * own.size),
    )(*all_near((own, *arrived, *after)))


def shift(values, by):
    return lax.ppermute(values, "z", [(place, (place + by) % 8) for place in range(8)])


def swap(values, axis, size, bit):
    return lax.ppermute(values, axis, [(place, place ^ bit) for place in range(size)])


def shift(values, by):
    return lax.ppermute(values, "z", [(place, (place + by) % 8) for place in range(8)])


def local(pseudo_grad, error_buffer, basis_prev, master_weights, outer_momentum):
    core = lax.axis_index("core").astype(jnp.int32)
    rank = basis_prev.shape[1]
    grad, error = pseudo_grad[0], error_buffer[0]
    half = grad.shape[1] // 2
    which_mine, which_other = core.reshape(1), (1 - core).reshape(1)
    side = lax.axis_index("xh").astype(jnp.int32).reshape(1)
    depth = lax.axis_index("z").astype(jnp.int32).reshape(1)
    master, momentum = master_weights.T, outer_momentum.T

    given, merged_other, own = project(which_other, grad, error, basis_prev, jnp.bfloat16, master, momentum)
    received = swap(given, "core", 2, 1)
    across = swap(own, "xh", 2, 1)
    kept, merged_mine = project(which_mine, grad, error, basis_prev, jnp.float32, held=(merged_other,))
    merged = (merged_mine, merged_other)
    mine = combine(kept, received, merged)
    bundle = bundle_of(own, across)
    up, down = shift(bundle, 1), shift(bundle, -1)
    chunks = lax.all_to_all(mine.reshape(16, rank // 16, half), plane, 0, 0, tiled=True)
    block = sum_chunks(chunks, (up, down), merged)
    block, _ = add_after(block, swap(block, "z", 8, 1), [to_near(array) for array in merged])
    copies, (up, down) = spread(block, from_pairs(block), 16, (up, down))
    pieces = [bundle, up, down]
    up, down = pass_through((shift(up, 1), shift(down, -1)))
    pieces += [up, down]
    begun, token = gather_pieces(side, depth, [to_far(piece) for piece in pieces], (0, -1, 1, -2, 2))
    up, down = shift(up, 1), shift(down, -1)
    far_side = shift(up, 1)
    mine = lax.all_to_all(copies, plane, 0, 0, tiled=True)
    mine = pass_after(mine, (up, down, token, merged)).reshape(rank, half)
    other = swap(mine, "core", 2, 1)

    before, _ = product_of(merged_mine, mine)
    (product, gram_mat), _ = product_of(merged_other, other, before)

    inverse = inverse_factor(gram_mat, (mine, other, *merged))
    product = add_quad(product, from_quad(product), (inverse, mine, other, *merged))
    arrived = from_pairs(product)
    basis_bf, basis_block = basis_of(which_mine, side, depth, inverse, mine, other, master.shape[0], product)
    carried, _ = gather_pieces(
        side, depth, [*map(to_far, (*pieces[3:], up, down)), to_near(far_side)], (-2, 2, -3, 3, -4), (begun, product)
    )

    error_next, weights_next, master_next, momentum_next = final(
        16, which_mine, inverse, product, arrived, basis_bf, merged_mine, merged_other, carried, basis_block,
        master, momentum,
    )
    return (error_next[None], weights_next, master_next.T, momentum_next.T)


def solution(mesh):
    fine = Mesh(mesh.devices.reshape(2, 8, 4, 2, 2), island + fsdp)
    in_specs = (
        P(island, fsdp, None),
        P(island, fsdp, None),
        P(fsdp, None),
        P(fsdp, island),
        P(fsdp, island),
    )
    out_specs = (
        P(island, fsdp, None),
        P(fsdp, None),
        P(fsdp, island),
        P(fsdp, island),
    )
    return jax.shard_map(local, mesh=fine, in_specs=in_specs, out_specs=out_specs, check_vma=False)
```

```python
import functools

import jax
import jax.numpy as jnp
from jax import lax
from jax.experimental import pallas as pl
from jax.experimental.pallas import tpu as pltpu
from jax.sharding import Mesh, PartitionSpec as P

momentum_coef = 0.9
outer_rate = 0.7
momentum_part = outer_rate * momentum_coef * momentum_coef
approx_part = outer_rate * (1.0 + momentum_coef)

island = ("xh", "z")
fsdp = ("y", "xl", "core")
plane = ("xh", "y", "xl")
panel = 32
group = 16
whole = pl.BlockSpec(memory_space=pltpu.VMEM)
anywhere = pl.BlockSpec(memory_space=pl.ANY)
scalars = pl.BlockSpec(memory_space=pltpu.SMEM)


def to_bf(values):
    return values.astype(jnp.bfloat16)


def to_f32(values):
    return values.astype(jnp.float32)


def times(left_mat, right_mat, left_dim=1, right_dim=0, precision=None):
    return lax.dot_general(
        left_mat,
        right_mat,
        (((left_dim,), (right_dim,)), ((), ())),
        precision=precision,
        preferred_element_type=jnp.float32,
    )


def shaped(shape, dtype):
    return jax.ShapeDtypeStruct(shape, dtype)


def far(shape, dtype):
    return pltpu.HBM(shape, dtype)


def all_near(arrays):
    return [to_near(array) for array in arrays]


def near(shape, dtype):
    return pltpu.VMEM(shape, dtype)


def to_near(values):
    return pltpu.with_memory_space_constraint(values, pltpu.VMEM)


def to_far(values):
    return pltpu.with_memory_space_constraint(values, pltpu.HBM)


def params(size=16):
    return pltpu.CompilerParams(vmem_limit_bytes=size * 2**20)


def cost(flops, size):
    return pl.CostEstimate(flops=flops, bytes_accessed=size, transcendentals=0)


def fetch(source, target, sem):
    copy = pltpu.make_async_copy(source, target, sem)
    copy.start()
    return copy


def project_kernel(pieces, which, grad, error, basis, *rest):
    first = len(rest) > 7
    if first:
        master, momentum, left_out, merged_out, own_out, grads, errors, bases, sems, masters, momenta = rest
    else:
        left_out, merged_out, grads, errors, bases, sems = rest[-6:]
    half = left_out.shape[1]
    width = half // pieces
    start = which[0] * half
    waits = [fetch(basis, bases, sems.at[0])]
    for piece in range(pieces):
        there = pl.ds(pl.multiple_of(start + piece * width, width), width)
        here = pl.ds(piece * width, width)
        waits.append(fetch(grad.at[:, there], grads.at[:, here], sems.at[1 + 2 * piece]))
        waits.append(fetch(error.at[:, there], errors.at[:, here], sems.at[2 + 2 * piece]))
    if first:
        waits.append(fetch(master, masters, sems.at[1 + 2 * pieces]))
        waits.append(fetch(momentum, momenta, sems.at[2 + 2 * pieces]))
    waits[0].wait()
    turned = to_bf(to_f32(bases[...]).T)
    for piece in range(pieces):
        here = slice(piece * width, (piece + 1) * width)
        waits[1 + 2 * piece].wait()
        waits[2 + 2 * piece].wait()
        merged = to_bf(to_f32(grads[:, here]) + to_f32(errors[:, here]))
        merged_out[:, here] = merged
        left_out[:, here] = times(turned, merged).astype(left_out.dtype)
    if first:
        waits[-2].wait()
        waits[-1].wait()
        own_out[...] = to_bf(masters[...] - momentum_part * momenta[...])


def project(which, grad, error, basis, dtype, master=None, momentum=None, held=()):
    rows, cols = grad.shape
    rank = basis.shape[1]
    half = cols // 2
    pieces = 5
    out_shape = [near((rank, half), dtype), near((rows, half), jnp.bfloat16)]
    operands = [which, to_far(grad), to_far(error), to_far(basis)]
    scratch = [
        pltpu.VMEM((rows, half), jnp.bfloat16),
        pltpu.VMEM((rows, half), jnp.bfloat16),
        pltpu.VMEM((rows, rank), jnp.bfloat16),
        pltpu.SemaphoreType.DMA((3 + 2 * pieces,)),
    ]
    operands += all_near(held)
    if master is not None:
        operands += [to_far(master), to_far(momentum)]
        out_shape.append(near(master.shape, jnp.bfloat16))
        scratch += [pltpu.VMEM(master.shape, jnp.float32)] * 2
    return pl.pallas_call(
        functools.partial(project_kernel, pieces),
        in_specs=[scalars] + [anywhere] * (len(operands) - 1),
        out_specs=[whole] * len(out_shape),
        out_shape=out_shape,
        scratch_shapes=scratch,
        compiler_params=params(24),
        cost_estimate=cost(rows * cols * rank, 2 * rows * cols),
    )(*operands)


def combine_kernel(kept, received, *rest):
    rest[-1][...] = to_bf(kept[...] + to_f32(received[...]))


def combine(kept, received, held):
    return pl.pallas_call(
        combine_kernel,
        in_specs=[whole] * 2 + [anywhere] * len(held),
        out_specs=whole,
        out_shape=shaped(kept.shape, jnp.bfloat16),
        compiler_params=params(),
        cost_estimate=cost(kept.size, 8 * kept.size),
    )(to_near(kept), to_near(received), *all_near(held))


def bundle_kernel(own, across, out):
    out[0] = own[...]
    out[1] = across[...]


def bundle_of(own, across):
    return pl.pallas_call(
        bundle_kernel,
        in_specs=[whole] * 2,
        out_specs=whole,
        out_shape=far((2,) + own.shape, own.dtype),
        compiler_params=params(),
        cost_estimate=cost(10**11, own.size),
    )(to_near(own), to_near(across))


def sum_kernel(chunks, *rest):
    out = rest[-1]
    total = to_f32(chunks[0])
    for place in range(1, chunks.shape[0]):
        total = total + to_f32(chunks[place])
    out[...] = to_bf(total)


def sum_chunks(chunks, after, held):
    return pl.pallas_call(
        sum_kernel,
        in_specs=[whole] + [anywhere] * (len(after) + len(held)),
        out_specs=whole,
        out_shape=near(chunks.shape[1:], jnp.bfloat16),
        compiler_params=params(),
        cost_estimate=cost(chunks.size, 2 * chunks.size),
    )(to_near(chunks), *[to_far(array) for array in after], *all_near(held))


def sum_pairs(own, opposite, before, after):
    return (to_f32(own[...]) + to_f32(opposite[...])) + (to_f32(before[...]) + to_f32(after[...]))


def spread_kernel(count, block, before, after, opposite, *rest):
    out = rest[-1]
    total = to_bf(sum_pairs(block, opposite, before, after))
    for place in range(count):
        out[place] = total


def spread(block, arrived, count, held):
    outs = pl.pallas_call(
        functools.partial(spread_kernel, count),
        in_specs=[whole] * 4 + [anywhere] * len(held),
        out_specs=[anywhere] * len(held) + [whole],
        out_shape=[far(array.shape, array.dtype) for array in held]
        + [far((count,) + block.shape, jnp.bfloat16)],
        input_output_aliases={4 + place: place for place in range(len(held))},
        compiler_params=params(),
        cost_estimate=cost(10**11, 2 * count * block.size),
    )(*[to_near(array) for array in (block, *arrived)], *[to_far(array) for array in held])
    return outs[-1], outs[:-1]


def product_kernel(first, merged, left, *rest):
    values = left[...]
    product = times(merged[...], values, 1, 1)
    gram_mat = times(values, values, 1, 1)
    product_out, gram_out = rest[-2:]
    if not first:
        product = rest[0][...] + product
        gram_mat = rest[1][...] + gram_mat
    product_out[...] = product.astype(product_out.dtype)
    gram_out[...] = gram_mat


def product_of(merged, left, before=(), held=()):
    rows = merged.shape[0]
    rank = left.shape[0]
    outs = pl.pallas_call(
        functools.partial(product_kernel, not before),
        in_specs=[whole] * (2 + len(before)) + [anywhere] * len(held),
        out_specs=[anywhere] * len(held) + [whole] * 2,
        out_shape=[far(array.shape, array.dtype) for array in held]
        + [near((rows, rank), jnp.bfloat16 if before else jnp.float32), near((rank, rank), jnp.float32)],
        input_output_aliases={2 + len(before) + place: place for place in range(len(held))},
        compiler_params=params(),
        cost_estimate=cost(2 * rows * left.size, 4 * left.size),
    )(to_near(merged), to_near(left), *[to_near(array) for array in before], *[to_far(array) for array in held])
    return outs[-2:], outs[:-2]


def factor_kernel(gram_mat, *refs):
    inverse_out, state, below_all = refs[-3:]
    rank = gram_mat.shape[0]
    exact = lax.Precision.HIGHEST
    row_of = lax.broadcasted_iota(jnp.int32, (rank, rank), 0)
    col_of = lax.broadcasted_iota(jnp.int32, (rank, rank), 1)
    state[...] = gram_mat[...]
    below_all[...] = jnp.where(row_of == col_of, 1.0, 0.0)
    row_of, col_of = row_of[:panel], col_of[:panel]
    for start in range(0, rank, panel):
        stop = start + panel
        rows, below = state[start:stop, :], below_all[start:stop, :]
        for first in range(0, panel, group):
            columns = [
                jnp.broadcast_to(rows[:, start + k : start + k + 1], (panel, rank))
                for k in range(first, first + group)
            ]
            for place in range(group):
                k = first + place
                factor = jnp.where(row_of > k, columns[place], 0.0) * (1.0 / columns[place][k : k + 1, :])
                for later in range(place + 1, group):
                    columns[later] = columns[later] - factor * columns[later][k : k + 1, :]
                rows = rows - factor * rows[k : k + 1, :]
                below = below - factor * below[k : k + 1, :]
        diagonal = jnp.sum(jnp.where(col_of == row_of + start, rows, 0.0), axis=1, keepdims=True)
        scale = lax.rsqrt(diagonal)
        rows, below = rows * scale, below * scale
        inverse_out[start:stop, :] = below
        if stop < rank:
            later = rows.T[stop:, :]
            state[stop:, :] -= times(later, rows, precision=exact)
            below_all[stop:, :] -= times(later, below, precision=exact)


def inverse_factor(gram_mat, kept):
    rank = gram_mat.shape[0]
    return pl.pallas_call(
        factor_kernel,
        in_specs=[whole] + [anywhere] * len(kept),
        out_specs=whole,
        out_shape=near((rank, rank), jnp.float32),
        scratch_shapes=[pltpu.VMEM((rank, rank), jnp.float32)] * 2,
        compiler_params=params(),
        cost_estimate=cost(10**9, 4 * rank * rank * 4),
    )(to_near(gram_mat), *[to_near(array) for array in kept])


def basis_kernel(which, side, depth, inverse, mine, other, _, out, block_out, held):
    half = mine.shape[1]
    value = inverse[...]
    high = to_bf(value)
    low = to_bf(value - to_f32(high))

    def put(left, start):
        left = left[...]
        basis = times(high, left) + times(low, left)
        out[:, pl.ds(pl.multiple_of(start, half), half)] = to_bf(basis)

    put(mine, which[0] * half)
    put(other, (1 - which[0]) * half)
    size = block_out.shape[0]
    pair = side[0] * half + (depth[0] // 2) * (2 * size)
    held[...] = to_f32(out[:, pl.ds(pl.multiple_of(pair, 2 * size), 2 * size)]).T
    block_out[...] = to_bf(held[pl.ds(pl.multiple_of(lax.rem(depth[0], 2) * size, size), size), :])


def basis_of(which, side, depth, inverse, mine, other, size, after):
    rank, half = mine.shape
    return pl.pallas_call(
        basis_kernel,
        in_specs=[scalars] * 3 + [whole] * 3 + [anywhere],
        out_specs=[whole] * 2,
        out_shape=[near((rank, 2 * half), jnp.bfloat16), near((size, rank), jnp.bfloat16)],
        scratch_shapes=[pltpu.VMEM((2 * size, rank), jnp.float32)],
        compiler_params=params(),
        cost_estimate=cost(8 * rank * rank * half, 8 * rank * half),
    )(which, side, depth, to_near(inverse), to_near(mine), to_near(other), after)


def final_kernel(
    islands, pieces, which, inverse, product, before, after, opposite, basis, merged_mine, merged_other, carried, block, master,
    momentum, error_out, weights_out, master_out, momentum_out, errors, weights, masters, momenta, sems,
):
    total = sum_pairs(product, opposite, before, after)
    q_avg = to_bf(times(total, inverse[...], 1, 1, lax.Precision.HIGHEST) / islands)
    half = merged_mine.shape[1]
    width = half // pieces
    waits = []
    for number, merged in enumerate((merged_mine, merged_other)):
        start = lax.rem(which[0] + number, 2) * half
        for piece in range(pieces):
            lanes = pl.ds(pl.multiple_of(start + piece * width, width), width)
            approx = times(q_avg, basis[:, lanes])
            errors[:, lanes] = to_bf(to_f32(merged[:, piece * width : (piece + 1) * width]) - approx)
            waits.append(fetch(errors.at[:, lanes], error_out.at[:, lanes], sems.at[len(waits)]))
            weights[:, lanes] = to_bf(to_f32(carried[:, lanes]) - approx_part * approx)
            waits.append(fetch(weights.at[:, lanes], weights_out.at[:, lanes], sems.at[len(waits)]))
    update = times(block[...], q_avg, 1, 1)
    momentum_next = momentum_coef * momentum[...] + update
    momenta[...] = momentum_next
    waits.append(fetch(momenta, momentum_out, sems.at[len(waits)]))
    masters[...] = master[...] - outer_rate * (update + momentum_coef * momentum_next)
    waits.append(fetch(masters, master_out, sems.at[len(waits)]))
    for copy in waits:
        copy.wait()


def final(islands, which, inverse, product, arrived, basis, mine, other, carried, block, master, momentum):
    rows, half = mine.shape
    rank = basis.shape[0]
    cols = 2 * half
    own = master.shape
    pieces = 5
    return pl.pallas_call(
        functools.partial(final_kernel, islands, pieces),
        in_specs=[scalars] + [whole] * 12,
        out_specs=[anywhere] * 4,
        out_shape=[
            shaped((rows, cols), jnp.bfloat16),
            shaped((rows, cols), jnp.bfloat16),
            shaped(own, jnp.float32),
            shaped(own, jnp.float32),
        ],
        scratch_shapes=[pltpu.VMEM((rows, cols), jnp.bfloat16)] * 2
        + [pltpu.VMEM(own, jnp.float32)] * 2
        + [pltpu.SemaphoreType.DMA((4 * pieces + 2,))],
        compiler_params=params(24),
        cost_estimate=cost(2 * rows * cols * rank, 8 * rows * cols),
    )(
        which, to_near(inverse), *[to_near(array) for array in (product, *arrived)], to_near(basis), to_near(mine), to_near(other),
        to_near(carried), to_near(block), master, momentum,
    )


def gather_kernel(shifts, side_of, depth, *refs):
    count = len(shifts)
    pieces, out, token, held, sems = refs[:count], *refs[-4:]
    token[...] = jnp.zeros_like(token)
    size = pieces[0].shape[1]
    ring = held.shape[1] // size
    waits = []
    for number in range(count):
        z_of = lax.rem(depth[0] + (shifts[number] + ring), ring)
        rows = pl.ds(pl.multiple_of(z_of * size, size), size)
        for half in range(2):
            waits.append(fetch(pieces[number].at[half], held.at[half, rows], sems.at[len(waits)]))
    for copy in waits:
        copy.wait()
    pairs = ring // 2
    own = depth[0] // 2
    beyond = own + lax.rem(depth[0], 2) * 2 + (pairs - 1)
    turn = 0 if len(refs) == count + 4 else 2
    span = ring * size
    for pair in (own, beyond):
        first = lax.rem(pair + turn, pairs) * (2 * size)
        for half in range(2):
            start = lax.rem(side_of[0] + half, 2) * span
            lanes = pl.ds(pl.multiple_of(start + first, 2 * size), 2 * size)
            rows = pl.ds(pl.multiple_of(first, 2 * size), 2 * size)
            out[:, lanes] = to_bf(to_f32(held[half, rows, :]).T)


def gather_pieces(side, depth, pieces, shifts, before=()):
    rows, cols = pieces[0].shape[1:]
    count = len(pieces)
    ring = 8
    return pl.pallas_call(
        functools.partial(gather_kernel, shifts),
        in_specs=[scalars] * 2 + [anywhere] * count + ([whole, anywhere] if before else []),
        out_specs=[whole] * 2,
        out_shape=[near((cols, 2 * ring * rows), jnp.bfloat16), near((8, 128), jnp.float32)],
        scratch_shapes=[
            pltpu.VMEM((2, ring * rows, cols), jnp.bfloat16),
            pltpu.SemaphoreType.DMA((2 * count,)),
        ],
        input_output_aliases={2 + count: 0} if before else {},
        compiler_params=params(),
        cost_estimate=cost(10**9, 4 * count * rows * cols),
    )(side, depth, *pieces, *all_near(before))


def pass_kernel(*refs):
    pass


def pass_through(arrays):
    return pl.pallas_call(
        pass_kernel,
        in_specs=[anywhere] * len(arrays),
        out_specs=[anywhere] * len(arrays),
        out_shape=[far(array.shape, array.dtype) for array in arrays],
        input_output_aliases={place: place for place in range(len(arrays))},
        compiler_params=params(),
        cost_estimate=cost(10**11, 1),
    )(*[to_far(array) for array in arrays])


def pass_after(values, after):
    return pl.pallas_call(
        pass_kernel,
        in_specs=[anywhere] * (len(after) + len(after[-1])),
        out_specs=anywhere,
        out_shape=shaped(values.shape, values.dtype),
        input_output_aliases={0: 0},
        compiler_params=params(),
        cost_estimate=cost(1, 1),
    )(values, *after[:-1], *all_near(after[-1]))


def add_kernel(first, second, *rest):
    rest[-1][...] = to_bf(to_f32(first[...]) + to_f32(second[...]))


def add_after(first, second, after, held=()):
    outs = pl.pallas_call(
        add_kernel,
        in_specs=[whole, whole] + [anywhere] * (len(after) + len(held)),
        out_specs=[anywhere] * len(held) + [whole],
        out_shape=[far(array.shape, array.dtype) for array in held] + [near(first.shape, first.dtype)],
        input_output_aliases={2 + len(after) + place: place for place in range(len(held))},
        compiler_params=params(),
        cost_estimate=cost(first.size, 12 * first.size),
    )(to_near(first), to_near(second), *after, *[to_far(array) for array in held])
    return outs[-1], outs[:-1]


def from_pairs(values):
    evens, odds = range(0, 8, 2), range(1, 8, 2)

    def send(even_by, odd_by):
        routes = [(place, (place + even_by) % 8) for place in evens]
        return lax.ppermute(values, "z", routes + [(place, (place + odd_by) % 8) for place in odds])

    before = send(-1, 1)
    after = send(-2, 2)
    return before, after, send(-3, 3)


def from_quad(values):
    def send(mask):
        return lax.ppermute(values, island, [(place, place ^ mask) for place in range(16)])

    beside = send(1)
    across = send(8)
    return beside, across, send(9)


def add_quad_kernel(own, beside, across, corner, *rest):
    rest[-1][...] = to_bf(sum_pairs(own, across, beside, corner))


def add_quad(own, arrived, after):
    return pl.pallas_call(
        add_quad_kernel,
        in_specs=[whole] * 4 + [anywhere] * len(after),
        out_specs=whole,
        out_shape=near(own.shape, own.dtype),
        compiler_params=params(),
        cost_estimate=cost(own.size, 12 * own.size),
    )(*all_near((own, *arrived, *after)))


def shift(values, by):
    return lax.ppermute(values, "z", [(place, (place + by) % 8) for place in range(8)])


def swap(values, axis, size, bit):
    return lax.ppermute(values, axis, [(place, place ^ bit) for place in range(size)])


def local(pseudo_grad, error_buffer, basis_prev, master_weights, outer_momentum):
    core = lax.axis_index("core").astype(jnp.int32)
    rank = basis_prev.shape[1]
    grad, error = pseudo_grad[0], error_buffer[0]
    half = grad.shape[1] // 2
    which_mine, which_other = core.reshape(1), (1 - core).reshape(1)
    side = lax.axis_index("xh").astype(jnp.int32).reshape(1)
    depth = lax.axis_index("z").astype(jnp.int32).reshape(1)
    master, momentum = master_weights.T, outer_momentum.T

    given, merged_other, own = project(which_other, grad, error, basis_prev, jnp.bfloat16, master, momentum)
    received = swap(given, "core", 2, 1)
    across = swap(own, "xh", 2, 1)
    kept, merged_mine = project(which_mine, grad, error, basis_prev, jnp.float32, held=(merged_other,))
    merged = (merged_mine, merged_other)
    mine = combine(kept, received, merged)
    bundle = bundle_of(own, across)
    up, down = shift(bundle, 1), shift(bundle, -1)
    chunks = lax.all_to_all(mine.reshape(16, rank // 16, half), plane, 0, 0, tiled=True)
    block = sum_chunks(chunks, (up, down), merged)
    block, (up, down) = add_after(
        block, swap(block, "z", 8, 1), [to_near(array) for array in merged], (up, down)
    )
    copies, _ = spread(block, from_pairs(block), 16, ())
    pieces = [bundle, up, down]
    up, down = pass_through((shift(up, 1), shift(down, -1)))
    pieces += [up, down]
    begun, token = gather_pieces(side, depth, [to_far(piece) for piece in pieces], (0, -1, 1, -2, 2))
    up, down = shift(up, 1), shift(down, -1)
    far_side = shift(up, 1)
    mine = lax.all_to_all(copies, plane, 0, 0, tiled=True)
    mine = pass_after(mine, (up, token, merged)).reshape(rank, half)
    other = swap(mine, "core", 2, 1)

    before, _ = product_of(merged_mine, mine)
    (product, gram_mat), _ = product_of(merged_other, other, before)

    inverse = inverse_factor(gram_mat, (mine, other, *merged))
    product = add_quad(product, from_quad(product), (inverse, mine, other, down, *merged))
    arrived = from_pairs(product)
    basis_bf, basis_block = basis_of(which_mine, side, depth, inverse, mine, other, master.shape[0], product)
    carried, _ = gather_pieces(
        side, depth, [*map(to_far, pieces[3:]), *all_near((up, down, far_side))], (-2, 2, -3, 3, -4), (begun, product)
    )

    error_next, weights_next, master_next, momentum_next = final(
        16, which_mine, inverse, product, arrived, basis_bf, merged_mine, merged_other, carried, basis_block,
        master, momentum,
    )
    return (error_next[None], weights_next, master_next.T, momentum_next.T)


def solution(mesh):
    fine = Mesh(mesh.devices.reshape(2, 8, 4, 2, 2), island + fsdp)
    in_specs = (
        P(island, fsdp, None),
        P(island, fsdp, None),
        P(fsdp, None),
        P(fsdp, island),
        P(fsdp, island),
    )
    out_specs = (
        P(island, fsdp, None),
        P(fsdp, None),
        P(fsdp, island),
        P(fsdp, island),
    )
    return jax.shard_map(local, mesh=fine, in_specs=in_specs, out_specs=out_specs, check_vma=False)
```

```python
import functools

import jax
import jax.numpy as jnp
from jax import lax
from jax.experimental import pallas as pl
from jax.experimental.pallas import tpu as pltpu
from jax.sharding import Mesh, PartitionSpec as P

momentum_coef = 0.9
outer_rate = 0.7
momentum_part = outer_rate * momentum_coef * momentum_coef
approx_part = outer_rate * (1.0 + momentum_coef)

island = ("xh", "z")
fsdp = ("y", "xl", "core")
plane = ("xh", "y", "xl")
panel = 32
group = 16
whole = pl.BlockSpec(memory_space=pltpu.VMEM)
anywhere = pl.BlockSpec(memory_space=pl.ANY)
scalars = pl.BlockSpec(memory_space=pltpu.SMEM)


def to_bf(values):
    return values.astype(jnp.bfloat16)


def to_f32(values):
    return values.astype(jnp.float32)


def times(left_mat, right_mat, left_dim=1, right_dim=0, precision=None):
    return lax.dot_general(
        left_mat,
        right_mat,
        (((left_dim,), (right_dim,)), ((), ())),
        precision=precision,
        preferred_element_type=jnp.float32,
    )


def shaped(shape, dtype):
    return jax.ShapeDtypeStruct(shape, dtype)


def far(shape, dtype):
    return pltpu.HBM(shape, dtype)


def all_near(arrays):
    return [to_near(array) for array in arrays]


def near(shape, dtype):
    return pltpu.VMEM(shape, dtype)


def to_near(values):
    return pltpu.with_memory_space_constraint(values, pltpu.VMEM)


def to_far(values):
    return pltpu.with_memory_space_constraint(values, pltpu.HBM)


def params(size=16):
    return pltpu.CompilerParams(vmem_limit_bytes=size * 2**20)


def cost(flops, size):
    return pl.CostEstimate(flops=flops, bytes_accessed=size, transcendentals=0)


def fetch(source, target, sem):
    copy = pltpu.make_async_copy(source, target, sem)
    copy.start()
    return copy


def project_kernel(pieces, which, grad, error, basis, *rest):
    first = len(rest) > 7
    if first:
        master, momentum, left_out, merged_out, own_out, grads, errors, bases, sems, masters, momenta = rest
    else:
        left_out, merged_out, grads, errors, bases, sems = rest[-6:]
    half = left_out.shape[1]
    width = half // pieces
    start = which[0] * half
    waits = [fetch(basis, bases, sems.at[0])]
    for piece in range(pieces):
        there = pl.ds(pl.multiple_of(start + piece * width, width), width)
        here = pl.ds(piece * width, width)
        waits.append(fetch(grad.at[:, there], grads.at[:, here], sems.at[1 + 2 * piece]))
        waits.append(fetch(error.at[:, there], errors.at[:, here], sems.at[2 + 2 * piece]))
    if first:
        waits.append(fetch(master, masters, sems.at[1 + 2 * pieces]))
        waits.append(fetch(momentum, momenta, sems.at[2 + 2 * pieces]))
    waits[0].wait()
    turned = to_bf(to_f32(bases[...]).T)
    for piece in range(pieces):
        here = slice(piece * width, (piece + 1) * width)
        waits[1 + 2 * piece].wait()
        waits[2 + 2 * piece].wait()
        merged = to_bf(to_f32(grads[:, here]) + to_f32(errors[:, here]))
        merged_out[:, here] = merged
        left_out[:, here] = times(turned, merged).astype(left_out.dtype)
    if first:
        waits[-2].wait()
        waits[-1].wait()
        own_out[...] = to_bf(masters[...] - momentum_part * momenta[...])


def project(which, grad, error, basis, dtype, master=None, momentum=None, held=()):
    rows, cols = grad.shape
    rank = basis.shape[1]
    half = cols // 2
    pieces = 5
    out_shape = [near((rank, half), dtype), near((rows, half), jnp.bfloat16)]
    operands = [which, to_far(grad), to_far(error), to_far(basis)]
    scratch = [
        pltpu.VMEM((rows, half), jnp.bfloat16),
        pltpu.VMEM((rows, half), jnp.bfloat16),
        pltpu.VMEM((rows, rank), jnp.bfloat16),
        pltpu.SemaphoreType.DMA((3 + 2 * pieces,)),
    ]
    operands += all_near(held)
    if master is not None:
        operands += [to_far(master), to_far(momentum)]
        out_shape.append(near(master.shape, jnp.bfloat16))
        scratch += [pltpu.VMEM(master.shape, jnp.float32)] * 2
    return pl.pallas_call(
        functools.partial(project_kernel, pieces),
        in_specs=[scalars] + [anywhere] * (len(operands) - 1),
        out_specs=[whole] * len(out_shape),
        out_shape=out_shape,
        scratch_shapes=scratch,
        compiler_params=params(24),
        cost_estimate=cost(rows * cols * rank, 2 * rows * cols),
    )(*operands)


def combine_kernel(kept, received, *rest):
    rest[-1][...] = to_bf(kept[...] + to_f32(received[...]))


def combine(kept, received, held):
    return pl.pallas_call(
        combine_kernel,
        in_specs=[whole] * 2 + [anywhere] * len(held),
        out_specs=whole,
        out_shape=shaped(kept.shape, jnp.bfloat16),
        compiler_params=params(),
        cost_estimate=cost(kept.size, 8 * kept.size),
    )(to_near(kept), to_near(received), *all_near(held))


def bundle_kernel(own, across, out):
    out[0] = own[...]
    out[1] = across[...]


def bundle_of(own, across):
    return pl.pallas_call(
        bundle_kernel,
        in_specs=[whole] * 2,
        out_specs=whole,
        out_shape=far((2,) + own.shape, own.dtype),
        compiler_params=params(),
        cost_estimate=cost(10**11, own.size),
    )(to_near(own), to_near(across))


def sum_kernel(chunks, *rest):
    out = rest[-1]
    total = to_f32(chunks[0])
    for place in range(1, chunks.shape[0]):
        total = total + to_f32(chunks[place])
    out[...] = to_bf(total)


def sum_chunks(chunks, after, held):
    return pl.pallas_call(
        sum_kernel,
        in_specs=[whole] + [anywhere] * (len(after) + len(held)),
        out_specs=whole,
        out_shape=near(chunks.shape[1:], jnp.bfloat16),
        compiler_params=params(),
        cost_estimate=cost(chunks.size, 2 * chunks.size),
    )(to_near(chunks), *[to_far(array) for array in after], *all_near(held))


def sum_pairs(own, opposite, before, after):
    return (to_f32(own[...]) + to_f32(opposite[...])) + (to_f32(before[...]) + to_f32(after[...]))


def spread_kernel(count, block, before, after, opposite, *rest):
    out = rest[-1]
    total = to_bf(sum_pairs(block, opposite, before, after))
    for place in range(count):
        out[place] = total


def spread(block, arrived, count, held):
    outs = pl.pallas_call(
        functools.partial(spread_kernel, count),
        in_specs=[whole] * 4 + [anywhere] * len(held),
        out_specs=[anywhere] * len(held) + [whole],
        out_shape=[far(array.shape, array.dtype) for array in held]
        + [far((count,) + block.shape, jnp.bfloat16)],
        input_output_aliases={4 + place: place for place in range(len(held))},
        compiler_params=params(),
        cost_estimate=cost(10**11, 2 * count * block.size),
    )(*[to_near(array) for array in (block, *arrived)], *[to_far(array) for array in held])
    return outs[-1], outs[:-1]


def product_kernel(merged, left, *rest):
    product = times(merged[...], left[...], 1, 1)
    if len(rest) == 2:
        product = rest[0][...] + product
    rest[-1][...] = product.astype(rest[-1].dtype)


def product_of(merged, left, before=()):
    rows = merged.shape[0]
    rank = left.shape[0]
    return pl.pallas_call(
        product_kernel,
        in_specs=[whole] * (2 + len(before)),
        out_specs=whole,
        out_shape=near((rows, rank), jnp.bfloat16 if before else jnp.float32),
        compiler_params=params(),
        cost_estimate=cost(2 * rows * left.size, 4 * left.size),
    )(*all_near((merged, left, *before)))


def factor_kernel(mine, other, *refs):
    inverse_out, state, below_all = refs[-3:]
    rank = mine.shape[0]
    exact = lax.Precision.HIGHEST
    row_of = lax.broadcasted_iota(jnp.int32, (rank, rank), 0)
    col_of = lax.broadcasted_iota(jnp.int32, (rank, rank), 1)
    state[...] = times(mine[...], mine[...], 1, 1) + times(other[...], other[...], 1, 1)
    below_all[...] = jnp.where(row_of == col_of, 1.0, 0.0)
    row_of, col_of = row_of[:panel], col_of[:panel]
    for start in range(0, rank, panel):
        stop = start + panel
        rows, below = state[start:stop, :], below_all[start:stop, :]
        for first in range(0, panel, group):
            columns = [
                jnp.broadcast_to(rows[:, start + k : start + k + 1], (panel, rank))
                for k in range(first, first + group)
            ]
            for place in range(group):
                k = first + place
                factor = jnp.where(row_of > k, columns[place], 0.0) * (1.0 / columns[place][k : k + 1, :])
                for later in range(place + 1, group):
                    columns[later] = columns[later] - factor * columns[later][k : k + 1, :]
                rows = rows - factor * rows[k : k + 1, :]
                below = below - factor * below[k : k + 1, :]
        diagonal = jnp.sum(jnp.where(col_of == row_of + start, rows, 0.0), axis=1, keepdims=True)
        scale = lax.rsqrt(diagonal)
        rows, below = rows * scale, below * scale
        inverse_out[start:stop, :] = below
        if stop < rank:
            later = rows.T[stop:, :]
            state[stop:, :] -= times(later, rows, precision=exact)
            below_all[stop:, :] -= times(later, below, precision=exact)


def inverse_factor(mine, other, kept):
    rank = mine.shape[0]
    return pl.pallas_call(
        factor_kernel,
        in_specs=[whole] * 2 + [anywhere] * len(kept),
        out_specs=whole,
        out_shape=near((rank, rank), jnp.float32),
        scratch_shapes=[pltpu.VMEM((rank, rank), jnp.float32)] * 2,
        compiler_params=params(),
        cost_estimate=cost(10**9, 4 * rank * rank * 4),
    )(*all_near((mine, other, *kept)))


def basis_kernel(which, side, depth, inverse, mine, other, _, out, block_out, held):
    half = mine.shape[1]
    value = inverse[...]
    high = to_bf(value)
    low = to_bf(value - to_f32(high))

    def put(left, start):
        left = left[...]
        basis = times(high, left) + times(low, left)
        out[:, pl.ds(pl.multiple_of(start, half), half)] = to_bf(basis)

    put(mine, which[0] * half)
    put(other, (1 - which[0]) * half)
    size = block_out.shape[0]
    pair = side[0] * half + (depth[0] // 2) * (2 * size)
    held[...] = to_f32(out[:, pl.ds(pl.multiple_of(pair, 2 * size), 2 * size)]).T
    block_out[...] = to_bf(held[pl.ds(pl.multiple_of(lax.rem(depth[0], 2) * size, size), size), :])


def basis_of(which, side, depth, inverse, mine, other, size, after):
    rank, half = mine.shape
    return pl.pallas_call(
        basis_kernel,
        in_specs=[scalars] * 3 + [whole] * 3 + [anywhere],
        out_specs=[whole] * 2,
        out_shape=[near((rank, 2 * half), jnp.bfloat16), near((size, rank), jnp.bfloat16)],
        scratch_shapes=[pltpu.VMEM((2 * size, rank), jnp.float32)],
        compiler_params=params(),
        cost_estimate=cost(8 * rank * rank * half, 8 * rank * half),
    )(which, side, depth, to_near(inverse), to_near(mine), to_near(other), after)


def final_kernel(
    islands, pieces, which, inverse, product, before, after, opposite, basis, merged_mine, merged_other, carried, block, master,
    momentum, error_out, weights_out, master_out, momentum_out, errors, weights, masters, momenta, sems,
):
    total = sum_pairs(product, opposite, before, after)
    q_avg = to_bf(times(total, inverse[...], 1, 1, lax.Precision.HIGHEST) / islands)
    half = merged_mine.shape[1]
    width = half // pieces
    waits = []
    for number, merged in enumerate((merged_mine, merged_other)):
        start = lax.rem(which[0] + number, 2) * half
        for piece in range(pieces):
            lanes = pl.ds(pl.multiple_of(start + piece * width, width), width)
            approx = times(q_avg, basis[:, lanes])
            errors[:, lanes] = to_bf(to_f32(merged[:, piece * width : (piece + 1) * width]) - approx)
            waits.append(fetch(errors.at[:, lanes], error_out.at[:, lanes], sems.at[len(waits)]))
            weights[:, lanes] = to_bf(to_f32(carried[:, lanes]) - approx_part * approx)
            waits.append(fetch(weights.at[:, lanes], weights_out.at[:, lanes], sems.at[len(waits)]))
    update = times(block[...], q_avg, 1, 1)
    momentum_next = momentum_coef * momentum[...] + update
    momenta[...] = momentum_next
    waits.append(fetch(momenta, momentum_out, sems.at[len(waits)]))
    masters[...] = master[...] - outer_rate * (update + momentum_coef * momentum_next)
    waits.append(fetch(masters, master_out, sems.at[len(waits)]))
    for copy in waits:
        copy.wait()


def final(islands, which, inverse, product, arrived, basis, mine, other, carried, block, master, momentum):
    rows, half = mine.shape
    rank = basis.shape[0]
    cols = 2 * half
    own = master.shape
    pieces = 5
    return pl.pallas_call(
        functools.partial(final_kernel, islands, pieces),
        in_specs=[scalars] + [whole] * 12,
        out_specs=[anywhere] * 4,
        out_shape=[
            shaped((rows, cols), jnp.bfloat16),
            shaped((rows, cols), jnp.bfloat16),
            shaped(own, jnp.float32),
            shaped(own, jnp.float32),
        ],
        scratch_shapes=[pltpu.VMEM((rows, cols), jnp.bfloat16)] * 2
        + [pltpu.VMEM(own, jnp.float32)] * 2
        + [pltpu.SemaphoreType.DMA((4 * pieces + 2,))],
        compiler_params=params(24),
        cost_estimate=cost(2 * rows * cols * rank, 8 * rows * cols),
    )(
        which, to_near(inverse), *[to_near(array) for array in (product, *arrived)], to_near(basis), to_near(mine), to_near(other),
        to_near(carried), to_near(block), master, momentum,
    )


def gather_kernel(shifts, side_of, depth, *refs):
    count = len(shifts)
    pieces, out, token, held, sems = refs[:count], *refs[-4:]
    token[...] = jnp.zeros_like(token)
    size = pieces[0].shape[1]
    ring = held.shape[1] // size
    waits = []
    for number in range(count):
        z_of = lax.rem(depth[0] + (shifts[number] + ring), ring)
        rows = pl.ds(pl.multiple_of(z_of * size, size), size)
        for half in range(2):
            waits.append(fetch(pieces[number].at[half], held.at[half, rows], sems.at[len(waits)]))
    for copy in waits:
        copy.wait()
    pairs = ring // 2
    own = depth[0] // 2
    beyond = own + lax.rem(depth[0], 2) * 2 + (pairs - 1)
    turn = 0 if len(refs) == count + 4 else 2
    span = ring * size
    for pair in (own, beyond):
        first = lax.rem(pair + turn, pairs) * (2 * size)
        for half in range(2):
            start = lax.rem(side_of[0] + half, 2) * span
            lanes = pl.ds(pl.multiple_of(start + first, 2 * size), 2 * size)
            rows = pl.ds(pl.multiple_of(first, 2 * size), 2 * size)
            out[:, lanes] = to_bf(to_f32(held[half, rows, :]).T)


def gather_pieces(side, depth, pieces, shifts, before=()):
    rows, cols = pieces[0].shape[1:]
    count = len(pieces)
    ring = 8
    return pl.pallas_call(
        functools.partial(gather_kernel, shifts),
        in_specs=[scalars] * 2 + [anywhere] * count + ([whole, anywhere] if before else []),
        out_specs=[whole] * 2,
        out_shape=[near((cols, 2 * ring * rows), jnp.bfloat16), near((8, 128), jnp.float32)],
        scratch_shapes=[
            pltpu.VMEM((2, ring * rows, cols), jnp.bfloat16),
            pltpu.SemaphoreType.DMA((2 * count,)),
        ],
        input_output_aliases={2 + count: 0} if before else {},
        compiler_params=params(),
        cost_estimate=cost(10**9, 4 * count * rows * cols),
    )(side, depth, *pieces, *all_near(before))


def pass_kernel(*refs):
    pass


def pass_through(arrays):
    return pl.pallas_call(
        pass_kernel,
        in_specs=[anywhere] * len(arrays),
        out_specs=[anywhere] * len(arrays),
        out_shape=[far(array.shape, array.dtype) for array in arrays],
        input_output_aliases={place: place for place in range(len(arrays))},
        compiler_params=params(),
        cost_estimate=cost(10**11, 1),
    )(*[to_far(array) for array in arrays])


def pass_after(values, after):
    return pl.pallas_call(
        pass_kernel,
        in_specs=[anywhere] * (len(after) + len(after[-1])),
        out_specs=anywhere,
        out_shape=shaped(values.shape, values.dtype),
        input_output_aliases={0: 0},
        compiler_params=params(),
        cost_estimate=cost(1, 1),
    )(values, *after[:-1], *all_near(after[-1]))


def add_kernel(first, second, *rest):
    rest[-1][...] = to_bf(to_f32(first[...]) + to_f32(second[...]))


def add_after(first, second, after, held=()):
    outs = pl.pallas_call(
        add_kernel,
        in_specs=[whole, whole] + [anywhere] * (len(after) + len(held)),
        out_specs=[anywhere] * len(held) + [whole],
        out_shape=[far(array.shape, array.dtype) for array in held] + [near(first.shape, first.dtype)],
        input_output_aliases={2 + len(after) + place: place for place in range(len(held))},
        compiler_params=params(),
        cost_estimate=cost(first.size, 12 * first.size),
    )(to_near(first), to_near(second), *after, *[to_far(array) for array in held])
    return outs[-1], outs[:-1]


def from_pairs(values):
    evens, odds = range(0, 8, 2), range(1, 8, 2)

    def send(even_by, odd_by):
        routes = [(place, (place + even_by) % 8) for place in evens]
        return lax.ppermute(values, "z", routes + [(place, (place + odd_by) % 8) for place in odds])

    before = send(-1, 1)
    after = send(-2, 2)
    return before, after, send(-3, 3)


def from_quad(values):
    def send(mask):
        return lax.ppermute(values, island, [(place, place ^ mask) for place in range(16)])

    beside = send(1)
    across = send(8)
    return beside, across, send(9)


def add_quad_kernel(own, beside, across, corner, *rest):
    rest[-1][...] = to_bf(sum_pairs(own, across, beside, corner))


def add_quad(own, arrived, after):
    return pl.pallas_call(
        add_quad_kernel,
        in_specs=[whole] * 4 + [anywhere] * len(after),
        out_specs=whole,
        out_shape=near(own.shape, own.dtype),
        compiler_params=params(),
        cost_estimate=cost(own.size, 12 * own.size),
    )(*all_near((own, *arrived, *after)))


def shift(values, by):
    return lax.ppermute(values, "z", [(place, (place + by) % 8) for place in range(8)])


def swap(values, axis, size, bit):
    return lax.ppermute(values, axis, [(place, place ^ bit) for place in range(size)])


def local(pseudo_grad, error_buffer, basis_prev, master_weights, outer_momentum):
    core = lax.axis_index("core").astype(jnp.int32)
    rank = basis_prev.shape[1]
    grad, error = pseudo_grad[0], error_buffer[0]
    half = grad.shape[1] // 2
    which_mine, which_other = core.reshape(1), (1 - core).reshape(1)
    side = lax.axis_index("xh").astype(jnp.int32).reshape(1)
    depth = lax.axis_index("z").astype(jnp.int32).reshape(1)
    master, momentum = master_weights.T, outer_momentum.T

    given, merged_other, own = project(which_other, grad, error, basis_prev, jnp.bfloat16, master, momentum)
    received = swap(given, "core", 2, 1)
    across = swap(own, "xh", 2, 1)
    kept, merged_mine = project(which_mine, grad, error, basis_prev, jnp.float32, held=(merged_other,))
    merged = (merged_mine, merged_other)
    mine = combine(kept, received, merged)
    bundle = bundle_of(own, across)
    up, down = shift(bundle, 1), shift(bundle, -1)
    chunks = lax.all_to_all(mine.reshape(16, rank // 16, half), plane, 0, 0, tiled=True)
    block = sum_chunks(chunks, (up, down), merged)
    block, (up, down) = add_after(
        block, swap(block, "z", 8, 1), [to_near(array) for array in merged], (up, down)
    )
    copies, _ = spread(block, from_pairs(block), 16, ())
    pieces = [bundle, up, down]
    up, down = pass_through((shift(up, 1), shift(down, -1)))
    pieces += [up, down]
    begun, token = gather_pieces(side, depth, [to_far(piece) for piece in pieces], (0, -1, 1, -2, 2))
    up, down = shift(up, 1), shift(down, -1)
    far_side = shift(up, 1)
    mine = lax.all_to_all(copies, plane, 0, 0, tiled=True)
    mine = pass_after(mine, (up, token, merged)).reshape(rank, half)
    other = swap(mine, "core", 2, 1)

    product = product_of(merged_mine, mine)
    product = product_of(merged_other, other, (product,))

    inverse = inverse_factor(mine, other, merged)
    product = add_quad(product, from_quad(product), (inverse, mine, other, down, *merged))
    arrived = from_pairs(product)
    basis_bf, basis_block = basis_of(which_mine, side, depth, inverse, mine, other, master.shape[0], product)
    carried, _ = gather_pieces(
        side, depth, [*map(to_far, pieces[3:]), *all_near((up, down, far_side))], (-2, 2, -3, 3, -4), (begun, product)
    )

    error_next, weights_next, master_next, momentum_next = final(
        16, which_mine, inverse, product, arrived, basis_bf, merged_mine, merged_other, carried, basis_block,
        master, momentum,
    )
    return (error_next[None], weights_next, master_next.T, momentum_next.T)


def solution(mesh):
    fine = Mesh(mesh.devices.reshape(2, 8, 4, 2, 2), island + fsdp)
    in_specs = (
        P(island, fsdp, None),
        P(island, fsdp, None),
        P(fsdp, None),
        P(fsdp, island),
        P(fsdp, island),
    )
    out_specs = (
        P(island, fsdp, None),
        P(fsdp, None),
        P(fsdp, island),
        P(fsdp, island),
    )
    return jax.shard_map(local, mesh=fine, in_specs=in_specs, out_specs=out_specs, check_vma=False)
```
